256 devices in a mesh: pipe: 4 (over y_lo, core), ep: 64 (over y_hi, z, x).
Axes of the slice: x: 4, y: 4 (y_hi: 2, y_lo: 2; y = y_hi * 2 + y_lo), z: 8, core: 2. Of those that a mesh axis runs over, the one named last changes fastest.
Arguments:
- forward_inputs: bfloat16 [4, 8192, 3584], P('pipe', 'ep'), may hold values from -50 to 50
- forward_routes: int32 [4, 8192, 1], P('pipe', 'ep'), may hold values from 0 to 15; in each aligned block of 128 rows (0 to 127, 128 to 255, ..., all dimensions but the last counted through in order) at most 9 rows name the same one
- forward_gates: float32 [4, 8192, 1], P('pipe', 'ep'), may hold values from 0.1 to 1
- backward_inputs: bfloat16 [4, 8192, 3584], P('pipe', 'ep'), may hold values from -50 to 50
- backward_cotangent: bfloat16 [4, 8192, 3584], P('pipe', 'ep'), may hold values from -6 to 6
- backward_routes: int32 [4, 8192, 1], P('pipe', 'ep'), may hold values from 0 to 15; in each aligned block of 128 rows (0 to 127, 128 to 255, ..., all dimensions but the last counted through in order) at most 9 rows name the same one
- backward_gates: float32 [4, 8192, 1], P('pipe', 'ep'), may hold values from 0.1 to 1
- saved_preacts: bfloat16 [4, 64, 576, 512], P('pipe', 'ep'), may hold values from -6 to 6
- norm_gain: float32 [4, 3584], P('pipe'), may hold values from 0.1 to 1.9
- gate_weight: bfloat16 [4, 3584, 16384], P('pipe', None, 'ep'), may hold values from -0.09375 to 0.09375
- up_weight: bfloat16 [4, 3584, 16384], P('pipe', None, 'ep'), may hold values from -0.09375 to 0.09375
- down_weight: bfloat16 [4, 16384, 3584], P('pipe', 'ep'), may hold values from -0.1875 to 0.1875
Outputs:
- forward_outputs: bfloat16 [4, 8192, 3584], P('pipe', 'ep')
- input_grads: bfloat16 [4, 8192, 3584], P('pipe', 'ep')
The draws below stay inside these ranges and needn't reach their ends.
Inputs may be any that keep to these rules, and one draw needn't show every extreme that they name: `forward_routes`: each token names 1 different experts; in each section the rows of one device name any expert at most 9 times. `backward_routes`: each token names 1 different experts; in each section the rows of one device name any expert at most 9 times.
All inputs are finite; a program needn't handle non-finite values.
Results may differ from the reference program's by a relative error of at most 0.005.
Values may be sent and summed in bfloat16 or wider, within the bound.
A program may use at most 128 MiB of HBM per device.

```python
import math
from functools import partial
import jax
import jax.numpy as jnp
import numpy as np
from jax import lax

D = 3584
HID = 1024
SPLIT = 4
NODES_TOK = 1
TOK_DEV = 128
EXPERTS = 16
HID_DEV = 256
TOKENS = 8192
CAP = 9
N_PIPE = 4
N_EP = 64


def scaled_field(key, noise, row_low, row_high, column_low, column_high):
    row_key, column_key = jax.random.split(key, 2)
    row_scale = jnp.exp(jax.random.uniform(row_key, (N_PIPE, TOKENS, 1), jnp.float32, math.log(row_low), math.log(row_high)))
    column_scale = jnp.exp(jax.random.uniform(column_key, (1, 1, D), jnp.float32, math.log(column_low), math.log(column_high)))
    return (noise * row_scale * column_scale).astype(jnp.bfloat16)


def draw_forward_inputs(key, part):
    key = jax.random.fold_in(key, 11)
    noise_key = jax.random.fold_in(key, 1)
    noise = jnp.clip(jax.random.normal(noise_key, (N_PIPE, TOKENS, D), jnp.float32), -4.0, 4.0)
    return scaled_field(key, noise, 0.3, 3.0, 0.4, 4.0)


def draw_backward_inputs(key, part):
    key = jax.random.fold_in(key, 23)
    noise_key = jax.random.fold_in(key, 1)
    noise = jnp.clip(jax.random.normal(noise_key, (N_PIPE, TOKENS, D), jnp.float32), -4.0, 4.0)
    return scaled_field(key, noise, 0.3, 3.0, 0.4, 4.0)


def block_levels(rng, extent, pieces, least, largest):
    def one(dim, parts):
        heights = jax.random.uniform(jax.random.fold_in(jax.random.fold_in(rng, 6), dim), (parts,), jnp.float32, least / len(pieces), largest / len(pieces))
        return jnp.repeat(jnp.exp(heights), extent[dim] // parts).reshape((-1,) + (1,) * (len(extent) - dim - 1))

    gain = one(*pieces[0])
    for cut in pieces[1:]:
        gain = gain * one(*cut)
    return gain


def deal_out(rng, own, number, rows, count, top, most, lean):
    sequence = jax.random.permutation(rng, count)
    heavy_load, usual = portions_of(count, rows * top, most, lean, True), portions_of(count, rows * top, most, lean, False)
    places = jnp.arange(count)

    def named(lengths, rotation):
        used = int((lengths > 0).sum())
        fixed = max(1, used // 4)
        moved = fixed + (places - fixed + rotation * (used - fixed)) % max(1, count - fixed)
        return jnp.zeros((count,), jnp.int32).at[sequence[jnp.where(places < fixed, places, moved)]].set(jnp.asarray(lengths, jnp.int32))

    lengths = jnp.where(number % 4 == 0, named(heavy_load, number // 4), named(usual, number - number // 4 - 1))
    mixed = jax.random.permutation(jax.random.fold_in(own, 3), count)
    source_of, taker = mixed[0:count // 2 * 2:2], mixed[1:count // 2 * 2:2]
    margin = jnp.minimum(lengths[source_of] - 1, most - lengths[taker]) // 2
    margin = jnp.where((source_of == sequence[0]) | (taker == sequence[0]) | (lengths[taker] == 0), 0, jnp.maximum(margin, 0))
    moved = jax.random.randint(jax.random.fold_in(own, 4), (count // 2,), 0, 1 << 20) % (margin + 1)
    lengths = lengths.at[source_of].add(-moved).at[taker].add(moved)
    items = jnp.searchsorted(jnp.cumsum(lengths), jnp.arange(rows * top), side="right").astype(jnp.int32)
    listing = items.reshape(top, rows).T
    listing = listing[jax.random.permutation(jax.random.fold_in(own, 1), rows)]
    rotation = jax.random.randint(jax.random.fold_in(own, 2), (rows, 1), 0, top)
    return jnp.take_along_axis(listing, (jnp.arange(top)[None, :] + rotation) % top, axis=1)


def portions_of(count, total, reach, lean, full):
    portions = [(1 << 20) // math.isqrt(standing ** lean) + 1 for standing in range(1, count + 1)]
    largest = reach if full else min(reach, max(-(-total // count), total * portions[0] // sum(portions)))
    least = 1 if total - largest >= count - 1 else 0
    given, spare = [largest] + [least] * (count - 1), total - largest - least * (count - 1)
    while spare > 0:
        free = [i for i in range(1, count) if given[i] < largest] or [i for i in range(1, count) if given[i] < reach]
        mass, left = sum([portions[i] for i in free]), spare
        for i in free:
            addition = min(reach - given[i], max(1, left * portions[i] // mass), spare)
            given[i] = given[i] + addition
            spare = spare - addition
    return np.array(given)


def bell_draw(own_key, dims, scale, reach, shards=(), held_as=jnp.bfloat16):
    values = scale * jax.random.normal(own_key, dims, jnp.float32)
    if shards:
        values = values * block_levels(own_key, dims, shards, -0.22, 0.18)
    return jnp.clip(values, -reach, reach).astype(held_as)


def setup_inputs(seed: int = 0) -> dict:
    arg_keys = jax.random.split(jax.random.key(seed), 13)
    forward_inputs = draw_forward_inputs(jax.random.fold_in(arg_keys[12], 71), 0)
    forward_routes_keys = jax.random.split(jax.random.fold_in(arg_keys[1], 1), N_PIPE * TOKENS // TOK_DEV)
    forward_routes_turns = jax.random.permutation(jax.random.fold_in(arg_keys[1], 3), N_PIPE * TOKENS // TOK_DEV)
    forward_routes = jax.vmap(lambda own, number: deal_out(jax.random.fold_in(arg_keys[1], 2), own, number, TOK_DEV, EXPERTS, NODES_TOK, CAP, 2))(forward_routes_keys, forward_routes_turns).reshape((N_PIPE, TOKENS, NODES_TOK))
    forward_gates = jnp.clip(jnp.exp(math.log(1.0) - 2.3025851 * jax.random.uniform(arg_keys[2], (N_PIPE, TOKENS, NODES_TOK), jnp.float32) ** block_levels(arg_keys[2], (N_PIPE, TOKENS, NODES_TOK), ((0, 4), (1, 64)), -0.2, 0.2)), 0.1, 1.0)
    backward_inputs = draw_backward_inputs(jax.random.fold_in(arg_keys[12], 71), 0)
    backward_cotangent = bell_draw(arg_keys[4], (N_PIPE, TOKENS, D), 1.0, 6.0, ((0, 4), (1, 64)))
    backward_routes_keys = jax.random.split(jax.random.fold_in(arg_keys[5], 1), N_PIPE * TOKENS // TOK_DEV)
    backward_routes_turns = jax.random.permutation(jax.random.fold_in(arg_keys[5], 3), N_PIPE * TOKENS // TOK_DEV)
    backward_routes = jax.vmap(lambda own, number: deal_out(jax.random.fold_in(arg_keys[5], 2), own, number, TOK_DEV, EXPERTS, NODES_TOK, CAP, 2))(backward_routes_keys, backward_routes_turns).reshape((N_PIPE, TOKENS, NODES_TOK))
    backward_gates = jnp.clip(jnp.exp(math.log(1.0) - 2.3025851 * jax.random.uniform(arg_keys[6], (N_PIPE, TOKENS, NODES_TOK), jnp.float32) ** block_levels(arg_keys[6], (N_PIPE, TOKENS, NODES_TOK), ((0, 4), (1, 64)), -0.2, 0.2)), 0.1, 1.0)
    saved_preacts = bell_draw(arg_keys[7], (N_PIPE, N_EP, N_EP * CAP, 2 * HID_DEV), 1.0, 6.0, ((0, 4), (1, 64)))
    norm_gain = jnp.clip(1.0 + 0.18 * jax.random.normal(arg_keys[8], (N_PIPE, D), jnp.float32), 0.1, 1.9)
    gate_weight = bell_draw(arg_keys[9], (N_PIPE, D, EXPERTS * HID), D ** -0.5, 0.09375, ((0, 4), (2, 64)))
    up_weight = bell_draw(arg_keys[10], (N_PIPE, D, EXPERTS * HID), D ** -0.5, 0.09375, ((0, 4), (2, 64)))
    down_weight = bell_draw(arg_keys[11], (N_PIPE, EXPERTS * HID, D), HID ** -0.5, 0.1875, ((0, 4), (1, 64)))
    return dict(forward_inputs=forward_inputs, forward_routes=forward_routes, forward_gates=forward_gates, backward_inputs=backward_inputs, backward_cotangent=backward_cotangent, backward_routes=backward_routes, backward_gates=backward_gates, saved_preacts=saved_preacts, norm_gain=norm_gain, gate_weight=gate_weight, up_weight=up_weight, down_weight=down_weight)


epsilon = 1e-06

def device_routes(routes, split):
    widened = routes[:, :, None] * split + jnp.arange(split, dtype=jnp.int32)[None, None, :]
    return widened.reshape(routes.shape[0], -1).astype(jnp.int32)

def slot_rows(routes, capacity, groups):
    flattened = routes.reshape(-1)
    onehot = (flattened[:, None] == jnp.arange(groups, dtype=jnp.int32)[None, :]).astype(jnp.int32)
    before = jnp.cumsum(onehot, axis=0) - onehot
    return flattened * capacity + lax.optimization_barrier(jnp.sum(onehot * before, axis=1))

def pack_rows(slot_index, values, weights, capacity, groups, node_count):
    slot_total = groups * capacity
    pair_count = slot_index.shape[0]
    matches = slot_index[None, :] == jnp.arange(slot_total, dtype=jnp.int32)[:, None]
    filled = jnp.any(matches, axis=1)
    source = lax.optimization_barrier(jnp.sum(jnp.where(matches, jnp.arange(pair_count, dtype=jnp.int32)[None, :], 0), axis=1))
    picked = jnp.where(filled[:, None], values[source // node_count], jnp.zeros((), values.dtype))
    weight_rows = weights.reshape(pair_count, -1)[source]
    picked_weights = jnp.where(filled[:, None], weight_rows, jnp.zeros((), weights.dtype))
    return (picked.reshape(groups, capacity, -1), picked_weights.reshape(groups, capacity, -1))

def unit_rows(values, gain_row):
    widened = values.astype(jnp.float32)
    inverse = lax.rsqrt(lax.optimization_barrier(jnp.mean(widened * widened, axis=-1, keepdims=True)) + epsilon)
    return (widened * inverse * gain_row[None, :]).astype(jnp.bfloat16)

def dispatch(routes, values, weights):
    pair_count = NODES_TOK * SPLIT
    wide_routes = device_routes(routes, SPLIT)
    wide_weights = jnp.repeat(weights, SPLIT, axis=1)
    slot_index = jax.vmap(partial(slot_rows, capacity=CAP, groups=N_EP))(wide_routes.reshape(N_EP, TOK_DEV, pair_count))
    packer = partial(pack_rows, capacity=CAP, groups=N_EP, node_count=pair_count)
    packed, packed_weights = jax.vmap(packer)(slot_index, values.reshape(N_EP, TOK_DEV, -1), wide_weights.reshape(N_EP, TOK_DEV, -1))
    arrived = jnp.swapaxes(packed, 0, 1).reshape(N_EP, N_EP * CAP, -1)
    arrived_weights = jnp.swapaxes(packed_weights, 0, 1).reshape(N_EP, N_EP * CAP, -1)
    return (slot_index, arrived, arrived_weights)

def take_rows(source_rows, slot_index):
    return source_rows[slot_index]

def collect(slot_index, results):
    returned = jnp.swapaxes(results.reshape(N_EP, N_EP, CAP, -1), 0, 1).reshape(N_EP, N_EP * CAP, -1)
    picked = jax.vmap(take_rows)(returned, slot_index)
    return lax.optimization_barrier(jnp.sum(picked.astype(jnp.float32).reshape(TOKENS, NODES_TOK * SPLIT, -1), axis=1))

def experts_forward(items):
    rows_in, weights_in, gate_local, up_local, down_local = items
    pre_gate = jnp.dot(rows_in, gate_local, preferred_element_type=jnp.float32)
    pre_up = jnp.dot(rows_in, up_local, preferred_element_type=jnp.float32)
    hidden = (weights_in.astype(jnp.float32) * jax.nn.silu(pre_gate) * pre_up).astype(jnp.bfloat16)
    return jnp.dot(hidden, down_local, preferred_element_type=jnp.float32).astype(jnp.bfloat16)

def experts_backward(items):
    rows_in, weights_in, saved_rows, gate_local, up_local, down_local = items
    hidden_width = gate_local.shape[1]
    back_hidden = jnp.dot(rows_in, down_local.T, preferred_element_type=jnp.float32)
    grad_hidden = weights_in.astype(jnp.float32) * back_hidden
    preacts = saved_rows.astype(jnp.float32)
    pre_gate = preacts[:, :hidden_width]
    pre_up = preacts[:, hidden_width:]
    sigmoid = jax.nn.sigmoid(pre_gate)
    grad_gate = (grad_hidden * pre_up * sigmoid * (1.0 + pre_gate * (1.0 - sigmoid))).astype(jnp.bfloat16)
    grad_up = (grad_hidden * pre_gate * sigmoid).astype(jnp.bfloat16)
    summed = jnp.dot(grad_gate, gate_local.T, preferred_element_type=jnp.float32)
    summed = summed + jnp.dot(grad_up, up_local.T, preferred_element_type=jnp.float32)
    return summed.astype(jnp.bfloat16)

def norm_backward(kept_inputs, gain_row, grad_normed, returning):
    widened = kept_inputs.astype(jnp.float32)
    inverse = lax.rsqrt(lax.optimization_barrier(jnp.mean(widened * widened, axis=-1, keepdims=True)) + epsilon)
    normal_rows = widened * inverse
    scaled_grad = grad_normed * gain_row[None, :]
    inner_mean = lax.optimization_barrier(jnp.mean(scaled_grad * normal_rows, axis=-1, keepdims=True))
    return (returning.astype(jnp.float32) + inverse * (scaled_grad - normal_rows * inner_mean)).astype(jnp.bfloat16)

def section_pass(items):
    arriving, routes_f, gates_f, kept_inputs, returning, routes_b, gates_b, saved_section, gain_row, gate_section, up_section, down_section = items
    gate_split = jnp.transpose(gate_section.reshape(D, N_EP, HID_DEV), (1, 0, 2))
    up_split = jnp.transpose(up_section.reshape(D, N_EP, HID_DEV), (1, 0, 2))
    down_split = down_section.reshape(N_EP, HID_DEV, D)
    normed = unit_rows(arriving, gain_row)
    slots_f, sent_f, sent_weights_f = dispatch(routes_f, normed, gates_f.astype(jnp.bfloat16))
    results_f = lax.map(experts_forward, (sent_f, sent_weights_f, gate_split, up_split, down_split))
    expert_sum = collect(slots_f, results_f)
    produced = (arriving.astype(jnp.float32) + expert_sum).astype(jnp.bfloat16)
    slots_b, sent_b, sent_weights_b = dispatch(routes_b, returning, gates_b.astype(jnp.bfloat16))
    results_b = lax.map(experts_backward, (sent_b, sent_weights_b, saved_section, gate_split, up_split, down_split))
    grad_normed = collect(slots_b, results_b)
    input_grad = norm_backward(kept_inputs, gain_row, grad_normed, returning)
    return (produced, input_grad)

def reference(forward_inputs, forward_routes, forward_gates, backward_inputs, backward_cotangent, backward_routes, backward_gates, saved_preacts, norm_gain, gate_weight, up_weight, down_weight):
    arriving = jnp.roll(forward_inputs, 1, axis=0)
    returning = jnp.roll(backward_cotangent, -1, axis=0)
    outputs, grads_all = lax.map(section_pass, (arriving, forward_routes, forward_gates, backward_inputs, returning, backward_routes, backward_gates, saved_preacts, norm_gain, gate_weight, up_weight, down_weight))
    return (outputs, grads_all)
```

```python
import functools
import jax
import jax.numpy as jnp
from jax import lax
from jax.experimental import pallas as pl
from jax.experimental.pallas import tpu as pltpu
from jax.sharding import PartitionSpec as P


RING = 4
NEXP = 16
TOK = 128
D = 3584
HID = 256
CAP = 9
ROWS = NEXP * CAP
NCH = 2
NSUB = 7
HALF = NSUB * 128
BLK = 64
PACK = NEXP * BLK
EPS = 1e-6
MESH = pl.DeviceIdType.MESH
F32 = jnp.float32
BF16 = jnp.bfloat16


def iota(shape, dim):
    return lax.broadcasted_iota(jnp.int32, shape, dim)


def nn(a, b):
    return lax.dot_general(a, b, (((1,), (0,)), ((), ())), preferred_element_type=F32)


def nt(a, b):
    return lax.dot_general(a, b, (((1,), (1,)), ((), ())), preferred_element_type=F32)


def hot(mask):
    return jnp.where(mask, 1.0, 0.0).astype(BF16)


def slot_places(routes):
    t0, t1 = iota((TOK, TOK), 0), iota((TOK, TOK), 1)
    wide = jnp.broadcast_to(routes, (TOK, TOK)).astype(F32)
    row = jnp.sum(jnp.where(t0 == t1, wide, 0.0), axis=0, keepdims=True)
    same = wide == row
    col_before = jnp.sum(jnp.where(same & (t1 < t0), 1.0, 0.0), axis=1, keepdims=True)
    row_before = jnp.sum(jnp.where(same & (t0 < t1), 1.0, 0.0), axis=0, keepdims=True)
    col = routes.astype(F32) * BLK + col_before
    return (row * BLK + row_before).astype(jnp.int32), col.astype(jnp.int32)


def kernel(fin, cot, bin_hbm, routes_f, gates_f, routes_b, gates_b, saved_hbm, gain_ref, wg_hbm, wu_hbm, wd_hbm,
           out_f, out_b,
           arr, ret, kept, saved, wg, wu, wd, put, get_m, pack_m, unpack_m, normed, send, recv, xs, xb, hs, hf, gs,
           ghb, gj, tsend, tsum, tfin, rs_in, rs_left, rs_right, ys, gnorm,
           loc_sem, p_send, p_recv, w_send, w_recv, d_send, d_recv, a_send, a_recv, h_send, h_recv, g_send, g_recv,
           r_send, r_recv):
    p, ep = lax.axis_index("pipe"), lax.axis_index("ep")
    e, k = ep // RING, ep % RING
    right = (p, e * RING + (k + 1) % RING)
    left = (p, e * RING + (k + 3) % RING)
    opposite = (p, e * RING + (k + 2) % RING)
    after, before = ((p + 1) % 4, ep), ((p + 3) % 4, ep)
    ring = {1: right, 2: opposite, 3: left}
    pending = []

    def remote(src, dst, ssem, rsem, device):
        copy = pltpu.make_async_remote_copy(src_ref=src, dst_ref=dst, send_sem=ssem, recv_sem=rsem, device_id=device,
                                            device_id_type=MESH)
        copy.start()
        pending.append(copy)
        return copy

    loads = [pltpu.make_async_copy(a, b, loc_sem.at[i]) for i, (a, b) in enumerate(
        ((wd_hbm, wd.at[0]), (wg_hbm, wg), (wu_hbm, wu), (saved_hbm, saved), (bin_hbm, kept)))]
    for load in loads:
        load.start()

    barrier = pltpu.get_barrier_semaphore()

    def greet(d, carry):
        pl.semaphore_signal(barrier, inc=1, device_id=(p, (e + d) % NEXP * RING + k), device_id_type=MESH)
        return carry

    lax.fori_loop(1, NEXP, greet, 0)
    for device in (right, left, opposite, after, before):
        pl.semaphore_signal(barrier, inc=1, device_id=device, device_id_type=MESH)
    pl.semaphore_wait(barrier, NEXP - 1 + 5)

    pipe_f = remote(fin, arr, p_send.at[0], p_recv.at[0], after)
    pipe_b = remote(cot, ret, p_send.at[1], p_recv.at[1], before)
    HA, HB = pl.ds(0, HID // 2), pl.ds(HID // 2, HID // 2)
    w_ra = remote(wd_hbm.at[HA], wd.at[3, HA], w_send.at[0], w_recv.at[0], right)
    w_lb = remote(wd_hbm.at[HB], wd.at[1, HB], w_send.at[1], w_recv.at[1], left)
    w_rb = remote(wd_hbm.at[HB], wd.at[3, HB], w_send.at[2], w_recv.at[2], right)
    w_la = remote(wd_hbm.at[HA], wd.at[1, HA], w_send.at[3], w_recv.at[3], left)

    rows_f, cols_f = slot_places(routes_f[...])
    rows_b, cols_b = slot_places(routes_b[...])

    def put_matrix(i, places):
        def one(j, carry):
            put[i, :, pl.ds(pl.multiple_of(j * 128, 128), 128)] = hot(iota((PACK, TOK), 0) == places + j * CAP)
            return carry
        lax.fori_loop(0, NSUB, one, 0)

    def get_matrix(i, places):
        def one(j, carry):
            get_m[i, pl.ds(pl.multiple_of(j * 128, 128), 128), :] = hot(iota((TOK, PACK), 1) == places + j * CAP)
            return carry
        lax.fori_loop(0, NSUB, one, 0)

    def ninth(v):
        return (v * 57) >> 9

    put_matrix(0, rows_f)
    put_matrix(1, rows_b)

    def unpack_one(j, carry):
        r = iota((ROWS, PACK), 0)
        r9 = ninth(r)
        unpack_m[pl.ds(pl.multiple_of(j * ROWS, 16), ROWS), :] = hot(
            iota((ROWS, PACK), 1) == r9 * (BLK - CAP) + r + j * CAP)
        return carry
    lax.fori_loop(0, NSUB, unpack_one, 0)
    for j in range(NSUB):
        r = iota((PACK, ROWS), 1)
        r9 = ninth(r)
        pack_m[:, j * ROWS:(j + 1) * ROWS] = hot(iota((PACK, ROWS), 0) == r9 * (BLK - CAP) + r + j * CAP)

    def spread(i, c):
        s = 2 * i + c

        def one(d, carry):
            to = (e + d) % NEXP
            pltpu.make_async_remote_copy(
                src_ref=send.at[i, c, pl.ds(pl.multiple_of(to * BLK, BLK), BLK)],
                dst_ref=recv.at[i, c, pl.ds(pl.multiple_of(e * BLK, BLK), BLK)],
                send_sem=d_send.at[s], recv_sem=d_recv.at[s],
                device_id=(p, to * RING + k), device_id_type=MESH).start()
            return carry
        lax.fori_loop(1, NEXP, one, 0)
        own = pl.ds(pl.multiple_of(e * BLK, BLK), BLK)
        recv[i, c, own, :] = send[i, c, own, :]

    def whole(i, c):
        part = pl.ds(0, PACK - BLK)
        return pltpu.make_async_remote_copy(
            src_ref=send.at[i, c, part], dst_ref=recv.at[i, c, part],
            send_sem=d_send.at[2 * i + c], recv_sem=d_recv.at[2 * i + c], device_id=right, device_id_type=MESH)

    def half(c, h):
        return pl.ds((2 * c + h) * HALF, HALF)

    def col(c, h, j):
        return pl.ds(pl.multiple_of((2 * c + h) * HALF + j * 128, 128), 128)

    def dispatch(i, values):
        for c in range(NCH):
            stack = jnp.concatenate([
                jnp.concatenate([values[:, (2 * c + h) * HALF + j * 128:(2 * c + h) * HALF + (j + 1) * 128]
                                 for h in range(2)], axis=1) for j in range(NSUB)], axis=0)
            for m in range(4):
                part = pl.ds(m * 256, 256)
                send[i, c, part, :] = nn(put[i, part, :], stack).astype(BF16)
            spread(i, c)

    def unpack(i, c, target):
        def one(j, carry):
            got = nn(unpack_m[pl.ds(pl.multiple_of(j * ROWS, 16), ROWS), :], recv[i, c]).astype(BF16)
            target[:, col(c, 0, j)] = got[:, :128]
            target[:, col(c, 1, j)] = got[:, 128:]
            return carry
        lax.fori_loop(0, NSUB, one, 0)

    pipe_f.wait_recv()
    wide = arr[...].astype(F32)
    inverse = lax.rsqrt(jnp.mean(wide * wide, axis=-1, keepdims=True) + EPS)
    normed[...] = (wide * inverse * gain_ref[...]).astype(BF16)
    dispatch(0, normed)

    pipe_b.wait_recv()
    dispatch(1, ret)

    w_ra.wait_recv()
    w_f = remote(wd.at[3, HA], wd.at[2, HA], w_send.at[4], w_recv.at[4], right)
    w_lb.wait_recv()
    w_g = remote(wd.at[1, HB], wd.at[2, HB], w_send.at[5], w_recv.at[5], left)

    gathers = []
    for c in range(NCH):
        whole(0, c).wait_recv()
        unpack(0, c, xs.at[0])
        A, B = half(c, 0), half(c, 1)
        o = 6 * c
        x_ra = remote(xs.at[0, :, A], xs.at[3, :, A], a_send.at[o], a_recv.at[o], right)
        x_lb = remote(xs.at[0, :, B], xs.at[1, :, B], a_send.at[o + 1], a_recv.at[o + 1], left)
        x_rb = remote(xs.at[0, :, B], xs.at[3, :, B], a_send.at[o + 2], a_recv.at[o + 2], right)
        x_la = remote(xs.at[0, :, A], xs.at[1, :, A], a_send.at[o + 3], a_recv.at[o + 3], left)
        gathers.append((A, B, o, x_ra, x_lb, x_rb, x_la))

    for load in loads:
        load.wait()

    get_matrix(0, cols_f)
    get_matrix(1, cols_b)

    for c in range(NCH):
        whole(1, c).wait_recv()
        unpack(1, c, xb)

    def grad_hidden(r):
        return nt(xb[...], wd[r]).astype(BF16)

    def give_grad(r):
        gs[r - 1] = grad_hidden(r)
        return remote(gs.at[r - 1], ghb.at[RING - r], g_send.at[r - 1], g_recv.at[r - 1], ring[r])

    ghb[0] = grad_hidden(0)
    w_rb.wait_recv()
    g3 = give_grad(3)
    w_la.wait_recv()
    g1 = give_grad(1)

    x_fwd = []
    for A, B, o, x_ra, x_lb, x_rb, x_la in gathers:
        x_ra.wait_recv()
        x_f = remote(xs.at[3, :, A], xs.at[2, :, A], a_send.at[o + 4], a_recv.at[o + 4], right)
        x_lb.wait_recv()
        x_g = remote(xs.at[1, :, B], xs.at[2, :, B], a_send.at[o + 5], a_recv.at[o + 5], left)
        x_fwd.append((x_f, x_g))

    w_f.wait_recv()
    w_g.wait_recv()
    g2 = give_grad(2)

    def hidden(r):
        rows = xs[r]
        pre_gate = nn(rows, wg[...])
        pre_up = nn(rows, wu[...])
        return (pre_gate / (1.0 + jnp.exp(-pre_gate)) * pre_up).astype(BF16)

    def give_hidden(r):
        hs[r - 1] = hidden(r)
        return remote(hs.at[r - 1], hf.at[RING - r], h_send.at[r - 1], h_recv.at[r - 1], ring[r])

    hf[0] = hidden(0)

    def grad_group(r):
        group = (k + r) % RING
        q = iota((ROWS, NEXP * RING * CAP), 0)
        take = hot(iota((ROWS, NEXP * RING * CAP), 1) == ninth(q) * (RING - 1) * CAP + q + group * CAP)
        pre = nn(take, saved[...])
        gate, up = pre[:, :HID], pre[:, HID:]
        grad = ghb[r].astype(F32)
        sigma = 1.0 / (1.0 + jnp.exp(-gate))
        gj[r, :, :HID] = (grad * up * sigma * (1.0 + gate * (1.0 - sigma))).astype(BF16)
        gj[r, :, HID:] = (grad * gate * sigma).astype(BF16)

    grad_group(0)
    for r, copy in ((2, g2), (1, g1), (3, g3)):
        copy.wait_recv()
    for r in (2, 1, 3):
        grad_group(r)

    def partial(r, q):
        cols = pl.ds(q * HALF, HALF)
        return nt(gj[r, :, :HID], wg[cols, :]) + nt(gj[r, :, HID:], wu[cols, :])

    sums = []
    for q in range(2 * NCH):
        cols = pl.ds(q * HALF, HALF)
        near, far = (1, 3) if q % 2 == 0 else (3, 1)
        tsend[0, :, cols] = partial(2, q).astype(BF16)
        first = remote(tsend.at[0, :, cols], rs_in.at[:, cols], r_send.at[3 * q], r_recv.at[3 * q], ring[near])
        tsend[1, :, cols] = partial(far, q).astype(BF16)
        single_to = rs_right if far == 3 else rs_left
        single = remote(tsend.at[1, :, cols], single_to.at[:, cols], r_send.at[3 * q + 1], r_recv.at[3 * q + 1],
                        ring[far])
        tsend[2, :, cols] = partial(near, q).astype(BF16)
        tfin[:, cols] = partial(0, q)
        sums.append((q, cols, near, first, single))

    finals = []
    for q, cols, near, first, single in sums:
        first.wait_recv()
        tsum[:, cols] = (tsend[2, :, cols].astype(F32) + rs_in[:, cols].astype(F32)).astype(BF16)
        summed_to = rs_left if near == 1 else rs_right
        summed = remote(tsum.at[:, cols], summed_to.at[:, cols], r_send.at[3 * q + 2], r_recv.at[3 * q + 2],
                        ring[near])
        finals.append((cols, single, summed))

    for x_f, x_g in x_fwd:
        pass
    for A, B, o, x_ra, x_lb, x_rb, x_la in gathers:
        x_rb.wait_recv()
        x_la.wait_recv()
    h1 = give_hidden(1)
    h3 = give_hidden(3)
    for x_f, x_g in x_fwd:
        x_f.wait_recv()
        x_g.wait_recv()
    h2 = give_hidden(2)

    def give_back(i, c):
        for m in range(4):
            part = pl.ds(m * 256, 256)
            send[2 + i, c, part, :] = nn(pack_m[part, :], ys[i, c]).astype(BF16)
        spread(2 + i, c)

    for copy in (h1, h3, h2):
        copy.wait_recv()
    for c in range(NCH):
        for h in range(2):
            total = nn(hf[0], wd[0, :, half(c, h)])
            for r in range(1, RING):
                total = total + nn(hf[r], wd[r, :, half(c, h)])
            total = total.astype(BF16)
            for j in range(NSUB):
                ys[0, c, j * ROWS:(j + 1) * ROWS, h * 128:(h + 1) * 128] = total[:, j * 128:(j + 1) * 128]
        give_back(0, c)

    for c in range(NCH):
        for h in range(2):
            cols, single, summed = finals[2 * c + h]
            single.wait_recv()
            summed.wait_recv()
            total = tfin[:, cols] + rs_left[:, cols].astype(F32) + rs_right[:, cols].astype(F32)
            total = total.astype(BF16)
            for j in range(NSUB):
                ys[1, c, j * ROWS:(j + 1) * ROWS, h * 128:(h + 1) * 128] = total[:, j * 128:(j + 1) * 128]
        give_back(1, c)

    gate_f = gates_f[...].astype(BF16).astype(F32)
    gate_b = gates_b[...].astype(BF16).astype(F32)

    def home(i, c, use):
        def one(j, carry):
            got = nn(get_m[i, pl.ds(pl.multiple_of(j * TOK, TOK), TOK), :], recv[2 + i, c])
            use(col(c, 0, j), got[:, :128])
            use(col(c, 1, j), got[:, 128:])
            return carry
        lax.fori_loop(0, NSUB, one, 0)

    def add_forward(cols, got):
        out_f[:, cols] = (arr[:, cols].astype(F32) + gate_f * got).astype(BF16)

    for c in range(NCH):
        whole(2, c).wait_recv()
        home(0, c, add_forward)

    kept_wide = kept[...].astype(F32)
    inverse_b = lax.rsqrt(jnp.mean(kept_wide * kept_wide, axis=-1, keepdims=True) + EPS)

    def keep(cols, got):
        gnorm[:, cols] = gate_b * got * gain_ref[:, cols]

    for c in range(NCH):
        whole(3, c).wait_recv()
        home(1, c, keep)
    scaled = gnorm[...]
    xhat = kept[...].astype(F32) * inverse_b
    inner = jnp.mean(scaled * xhat, axis=-1, keepdims=True)
    out_b[...] = (ret[...].astype(F32) + inverse_b * (scaled - xhat * inner)).astype(BF16)

    for copy in pending:
        copy.wait_send()
    for i in range(4):
        for c in range(NCH):
            whole(i, c).wait_send()


def on_device(forward_inputs, forward_routes, forward_gates, backward_inputs, backward_cotangent, backward_routes,
              backward_gates, saved_preacts, norm_gain, gate_weight, up_weight, down_weight):
    vmem = pl.BlockSpec(memory_space=pltpu.VMEM)
    hbm = pl.BlockSpec(memory_space=pl.ANY)
    dma = pltpu.SemaphoreType.DMA
    out = jax.ShapeDtypeStruct((TOK, D), BF16)
    scratch = [
        pltpu.VMEM((TOK, D), BF16),
        pltpu.VMEM((TOK, D), BF16),
        pltpu.VMEM((TOK, D), BF16),
        pltpu.VMEM((RING * ROWS, 2 * HID), BF16),
        pltpu.VMEM((D, HID), BF16),
        pltpu.VMEM((D, HID), BF16),
        pltpu.VMEM((RING, HID, D), BF16),
        pltpu.VMEM((2, PACK, NSUB * TOK), BF16),
        pltpu.VMEM((2, NSUB * TOK, PACK), BF16),
        pltpu.VMEM((PACK, NSUB * ROWS), BF16),
        pltpu.VMEM((NSUB * ROWS, PACK), BF16),
        pltpu.VMEM((TOK, D), BF16),
        pltpu.VMEM((4, NCH, PACK, 256), BF16),
        pltpu.VMEM((4, NCH, PACK, 256), BF16),
        pltpu.VMEM((RING, ROWS, D), BF16),
        pltpu.VMEM((ROWS, D), BF16),
        pltpu.VMEM((RING - 1, ROWS, HID), BF16),
        pltpu.VMEM((RING, ROWS, HID), BF16),
        pltpu.VMEM((RING - 1, ROWS, HID), BF16),
        pltpu.VMEM((RING, ROWS, HID), BF16),
        pltpu.VMEM((RING, ROWS, 2 * HID), BF16),
        pltpu.VMEM((3, ROWS, D), BF16),
        pltpu.VMEM((ROWS, D), BF16),
        pltpu.VMEM((ROWS, D), F32),
        pltpu.VMEM((ROWS, D), BF16),
        pltpu.VMEM((ROWS, D), BF16),
        pltpu.VMEM((ROWS, D), BF16),
        pltpu.VMEM((2, NCH, NSUB * ROWS, 256), BF16),
        pltpu.VMEM((TOK, D), F32),
        dma((5,)), dma((2,)), dma((2,)), dma((6,)), dma((6,)), dma((8,)), dma((8,)), dma((12,)), dma((12,)),
        dma((3,)), dma((3,)), dma((3,)), dma((3,)), dma((12,)), dma((12,)),
    ]
    call = pl.pallas_call(
        kernel,
        out_shape=(out, out),
        in_specs=[hbm, hbm, hbm, vmem, vmem, vmem, vmem, hbm, vmem, hbm, hbm, hbm],
        out_specs=(vmem, vmem),
        scratch_shapes=scratch,
        compiler_params=pltpu.CompilerParams(collective_id=0, has_side_effects=True,
                                             vmem_limit_bytes=62 * 2 ** 20),
        cost_estimate=pl.CostEstimate(flops=10 ** 10, bytes_accessed=2 * 10 ** 7, transcendentals=10 ** 6),
    )
    outputs, grads = call(
        forward_inputs[0], backward_cotangent[0], backward_inputs[0], forward_routes[0], forward_gates[0],
        backward_routes[0], backward_gates[0], saved_preacts[0, 0], norm_gain, gate_weight[0], up_weight[0],
        down_weight[0])
    return outputs[None], grads[None]


def solution(mesh):
    tokens = P("pipe", "ep", None)
    in_specs = (tokens,) * 7 + (P("pipe", "ep", None, None), P("pipe", None), P("pipe", None, "ep"),
                                P("pipe", None, "ep"), tokens)
    return jax.shard_map(on_device, mesh=mesh, in_specs=in_specs, out_specs=(tokens, tokens), check_vma=False)
```

```python
import functools
import jax
import jax.numpy as jnp
from jax import lax
from jax.experimental import pallas as pl
from jax.experimental.pallas import tpu as pltpu
from jax.sharding import PartitionSpec as P


RING = 4
NEXP = 16
TOK = 128
D = 3584
HID = 256
CAP = 9
ROWS = NEXP * CAP
NCH = 2
NSUB = 7
HALF = NSUB * 128
BLK = 64
PACK = NEXP * BLK
EPS = 1e-6
MESH = pl.DeviceIdType.MESH
F32 = jnp.float32
BF16 = jnp.bfloat16


def iota(shape, dim):
    return lax.broadcasted_iota(jnp.int32, shape, dim)


def nn(a, b):
    return lax.dot_general(a, b, (((1,), (0,)), ((), ())), preferred_element_type=F32)


def nt(a, b):
    return lax.dot_general(a, b, (((1,), (1,)), ((), ())), preferred_element_type=F32)


def hot(mask):
    return jnp.where(mask, 1.0, 0.0).astype(BF16)


def as_column(row):
    t0, t1 = iota((TOK, TOK), 0), iota((TOK, TOK), 1)
    return jnp.sum(jnp.where(t0 == t1, jnp.broadcast_to(row, (TOK, TOK)), 0.0), axis=1, keepdims=True)


def slot_places(routes):
    t0, t1 = iota((TOK, TOK), 0), iota((TOK, TOK), 1)
    row = routes.astype(F32)
    column = as_column(row)
    same = column == row
    col_before = jnp.sum(jnp.where(same & (t1 < t0), 1.0, 0.0), axis=1, keepdims=True)
    row_before = jnp.sum(jnp.where(same & (t0 < t1), 1.0, 0.0), axis=0, keepdims=True)
    col = column * BLK + col_before
    return (row * BLK + row_before).astype(jnp.int32), col.astype(jnp.int32)


def kernel(fin, cot, bin_hbm, routes_f, gates_f, routes_b, gates_b, saved_hbm, gain_ref, wg_hbm, wu_hbm, wd_hbm,
           out_f, out_b,
           arr, ret, kept, saved, wg, wu, wd, put, get_m, pack_m, unpack_m, normed, send, recv, xs, xb, hs, hf, gs,
           ghb, factor, gj, tsend, tnear, tfin, rs_in, rs_left, rs_right, ys, gnorm,
           loc_sem, p_send, p_recv, w_send, w_recv, d_send, d_recv, a_send, a_recv, h_send, h_recv, g_send, g_recv,
           r_send, r_recv):
    p, ep = lax.axis_index("pipe"), lax.axis_index("ep")
    e, k = ep // RING, ep % RING
    right = (p, e * RING + (k + 1) % RING)
    left = (p, e * RING + (k + 3) % RING)
    opposite = (p, e * RING + (k + 2) % RING)
    after, before = ((p + 1) % 4, ep), ((p + 3) % 4, ep)
    ring = {1: right, 2: opposite, 3: left}
    pending = []

    def remote(src, dst, ssem, rsem, device):
        copy = pltpu.make_async_remote_copy(src_ref=src, dst_ref=dst, send_sem=ssem, recv_sem=rsem, device_id=device,
                                            device_id_type=MESH)
        copy.start()
        pending.append(copy)
        return copy

    loads = [pltpu.make_async_copy(a, b, loc_sem.at[i]) for i, (a, b) in enumerate(
        ((wd_hbm, wd.at[0]), (wg_hbm, wg), (wu_hbm, wu), (saved_hbm, saved), (bin_hbm, kept)))]
    for load in loads:
        load.start()

    barrier = pltpu.get_barrier_semaphore()

    def greet(d, carry):
        pl.semaphore_signal(barrier, inc=1, device_id=(p, (e + d) % NEXP * RING + k), device_id_type=MESH)
        return carry

    lax.fori_loop(1, NEXP, greet, 0)
    for device in (right, left, opposite, after, before):
        pl.semaphore_signal(barrier, inc=1, device_id=device, device_id_type=MESH)
    with jax.named_scope("barrier wait"):
        pl.semaphore_wait(barrier, NEXP - 1 + 5)

    pipe_f = remote(fin, arr, p_send.at[0], p_recv.at[0], after)
    HA, HB = pl.ds(0, HID // 2), pl.ds(HID // 2, HID // 2)
    w_ra = remote(wd_hbm.at[HA], wd.at[3, HA], w_send.at[0], w_recv.at[0], right)
    w_lb = remote(wd_hbm.at[HB], wd.at[1, HB], w_send.at[1], w_recv.at[1], left)
    w_rb = remote(wd_hbm.at[HB], wd.at[3, HB], w_send.at[2], w_recv.at[2], right)
    w_la = remote(wd_hbm.at[HA], wd.at[1, HA], w_send.at[3], w_recv.at[3], left)

    def put_matrix(i, places):
        def one(j, carry):
            put[i, :, pl.ds(pl.multiple_of(j * 128, 128), 128)] = hot(iota((PACK, TOK), 0) == places + j * CAP)
            return carry
        lax.fori_loop(0, NSUB, one, 0)

    def get_matrix(i, places):
        def one(j, carry):
            get_m[i, pl.ds(pl.multiple_of(j * 128, 128), 128), :] = hot(iota((TOK, PACK), 1) == places + j * CAP)
            return carry
        lax.fori_loop(0, NSUB, one, 0)

    def ninth(v):
        return (v * 57) >> 9

    def unpack_matrix():
        def one(j, carry):
            r = iota((ROWS, PACK), 0)
            unpack_m[pl.ds(pl.multiple_of(j * ROWS, 16), ROWS), :] = hot(
                iota((ROWS, PACK), 1) == ninth(r) * (BLK - CAP) + r + j * CAP)
            return carry
        lax.fori_loop(0, NSUB, one, 0)

    def pack_matrix():
        for j in range(NSUB):
            r = iota((PACK, ROWS), 1)
            pack_m[:, j * ROWS:(j + 1) * ROWS] = hot(
                iota((PACK, ROWS), 0) == ninth(r) * (BLK - CAP) + r + j * CAP)

    def spread(i, c):
        s = 2 * i + c

        def one(d, carry):
            to = (e + d) % NEXP
            pltpu.make_async_remote_copy(
                src_ref=send.at[i, c, pl.ds(pl.multiple_of(to * BLK, BLK), BLK)],
                dst_ref=recv.at[i, c, pl.ds(pl.multiple_of(e * BLK, BLK), BLK)],
                send_sem=d_send.at[s], recv_sem=d_recv.at[s],
                device_id=(p, to * RING + k), device_id_type=MESH).start()
            return carry
        lax.fori_loop(1, NEXP, one, 0)
        own = pl.ds(pl.multiple_of(e * BLK, BLK), BLK)
        recv[i, c, own, :] = send[i, c, own, :]

    def whole(i, c):
        part = pl.ds(0, PACK - BLK)
        return pltpu.make_async_remote_copy(
            src_ref=send.at[i, c, part], dst_ref=recv.at[i, c, part],
            send_sem=d_send.at[2 * i + c], recv_sem=d_recv.at[2 * i + c], device_id=right, device_id_type=MESH)

    def half(c, h):
        return pl.ds((2 * c + h) * HALF, HALF)

    def col(c, h, j):
        return pl.ds(pl.multiple_of((2 * c + h) * HALF + j * 128, 128), 128)

    def dispatch(i, values):
        for c in range(NCH):
            stack = jnp.concatenate([
                jnp.concatenate([values[:, (2 * c + h) * HALF + j * 128:(2 * c + h) * HALF + (j + 1) * 128]
                                 for h in range(2)], axis=1) for j in range(NSUB)], axis=0)
            for m in range(4):
                part = pl.ds(m * 256, 256)
                send[i, c, part, :] = nn(put[i, part, :], stack).astype(BF16)
            spread(i, c)

    def unpack(i, c, target):
        def one(j, carry):
            got = nn(unpack_m[pl.ds(pl.multiple_of(j * ROWS, 16), ROWS), :], recv[i, c]).astype(BF16)
            target[:, col(c, 0, j)] = got[:, :128]
            target[:, col(c, 1, j)] = got[:, 128:]
            return carry
        lax.fori_loop(0, NSUB, one, 0)

    def saved_factors(r):
        group = (k + r) % RING
        q = iota((ROWS, NEXP * RING * CAP), 0)
        take = hot(iota((ROWS, NEXP * RING * CAP), 1) == ninth(q) * (RING - 1) * CAP + q + group * CAP)
        pre = nn(take, saved[...])
        gate, up = pre[:, :HID], pre[:, HID:]
        sigma = 1.0 / (1.0 + jnp.exp(-gate))
        factor[r, :, :HID] = up * sigma * (1.0 + gate * (1.0 - sigma))
        factor[r, :, HID:] = gate * sigma

    rows_f, cols_f = slot_places(routes_f[...])
    rows_b, cols_b = slot_places(routes_b[...])
    put_matrix(0, rows_f)

    with jax.named_scope("pipe f wait"):
        pipe_f.wait_recv()
    pipe_b = remote(cot, ret, p_send.at[1], p_recv.at[1], before)
    wide = arr[...].astype(F32)
    inverse = lax.rsqrt(jnp.mean(wide * wide, axis=-1, keepdims=True) + EPS)
    normed[...] = (wide * inverse * gain_ref[...]).astype(BF16)
    with jax.named_scope("dispatch f"):
        dispatch(0, normed)

    put_matrix(1, rows_b)
    unpack_matrix()
    for load in loads:
        load.wait()
    with jax.named_scope("saved factors"):
        for r in range(RING):
            saved_factors(r)

    with jax.named_scope("pipe b wait"):
        pipe_b.wait_recv()
    with jax.named_scope("dispatch b"):
        dispatch(1, ret)

    with jax.named_scope("matrices"):
        pack_matrix()
        get_matrix(0, cols_f)
        get_matrix(1, cols_b)

    def gather(c):
        with jax.named_scope(f"f disp wait {c}"):
            whole(0, c).wait_recv()
        unpack(0, c, xs.at[0])
        A, B = half(c, 0), half(c, 1)
        o = 6 * c
        x_ra = remote(xs.at[0, :, A], xs.at[3, :, A], a_send.at[o], a_recv.at[o], right)
        x_lb = remote(xs.at[0, :, B], xs.at[1, :, B], a_send.at[o + 1], a_recv.at[o + 1], left)
        x_rb = remote(xs.at[0, :, B], xs.at[3, :, B], a_send.at[o + 2], a_recv.at[o + 2], right)
        x_la = remote(xs.at[0, :, A], xs.at[1, :, A], a_send.at[o + 3], a_recv.at[o + 3], left)
        return x_ra, x_lb, x_rb, x_la

    def gather_on(c, x_ra, x_lb):
        A, B = half(c, 0), half(c, 1)
        o = 6 * c
        with jax.named_scope(f"x ra wait {c}"):
            x_ra.wait_recv()
        x_f = remote(xs.at[3, :, A], xs.at[2, :, A], a_send.at[o + 4], a_recv.at[o + 4], right)
        with jax.named_scope(f"x lb wait {c}"):
            x_lb.wait_recv()
        x_g = remote(xs.at[1, :, B], xs.at[2, :, B], a_send.at[o + 5], a_recv.at[o + 5], left)
        return x_f, x_g

    def weights_on(part):
        size = HID // 4
        a, b = pl.ds(part * size, size), pl.ds(HID // 2 + part * size, size)
        o = 4 + 2 * part
        return (remote(wd.at[3, a], wd.at[2, a], w_send.at[o], w_recv.at[o], right),
                remote(wd.at[1, b], wd.at[2, b], w_send.at[o + 1], w_recv.at[o + 1], left))

    def grad_hidden(r):
        return nt(xb[...], wd[r]).astype(BF16)

    def give_grad(r):
        gs[r - 1] = grad_hidden(r)
        return remote(gs.at[r - 1], ghb.at[RING - r], g_send.at[r - 1], g_recv.at[r - 1], ring[r])

    def hidden(r):
        rows = xs[r]
        pre_gate = nn(rows, wg[...])
        pre_up = nn(rows, wu[...])
        return (pre_gate / (1.0 + jnp.exp(-pre_gate)) * pre_up).astype(BF16)

    def give_hidden(r):
        hs[r - 1] = hidden(r)
        return remote(hs.at[r - 1], hf.at[RING - r], h_send.at[r - 1], h_recv.at[r - 1], ring[r])

    gathers = [gather(c) for c in range(NCH)]
    x_fwd = [gather_on(0, *gathers[0][:2])]
    with jax.named_scope("hidden 0"):
        hf[0] = hidden(0)

    with jax.named_scope("b disp wait 0"):
        whole(1, 0).wait_recv()
    unpack(1, 0, xb)
    x_fwd.append(gather_on(1, *gathers[1][:2]))
    with jax.named_scope("wd wait"):
        w_ra.wait_recv()
        w_lb.wait_recv()
    w_on = [weights_on(0)]
    with jax.named_scope("b disp wait 1"):
        whole(1, 1).wait_recv()
    unpack(1, 1, xb)

    with jax.named_scope("wd rest wait"):
        w_rb.wait_recv()
        w_la.wait_recv()
    with jax.named_scope("gh 3 1 0"):
        g3 = give_grad(3)
        g1 = give_grad(1)
        ghb[0] = grad_hidden(0)
    with jax.named_scope("x rb la wait"):
        for x_ra, x_lb, x_rb, x_la in gathers:
            x_rb.wait_recv()
            x_la.wait_recv()
    with jax.named_scope("hidden 1 3"):
        h1 = give_hidden(1)
        h3 = give_hidden(3)
    with jax.named_scope("x fwd wait"):
        for x_f, x_g in x_fwd:
            x_f.wait_recv()
            x_g.wait_recv()
    with jax.named_scope("hidden 2"):
        h2 = give_hidden(2)
    w_on.append(weights_on(1))

    def grad_group(r):
        grad = ghb[r].astype(F32)
        gj[r, :, :HID] = (grad * factor[r, :, :HID]).astype(BF16)
        gj[r, :, HID:] = (grad * factor[r, :, HID:]).astype(BF16)

    def partial(r, q):
        cols = pl.ds(q * HALF, HALF)
        return nt(gj[r, :, :HID], wg[cols, :]) + nt(gj[r, :, HID:], wu[cols, :])

    quarters = [pl.ds(q * HALF, HALF) for q in range(2 * NCH)]
    near = [1 if q % 2 == 0 else 3 for q in range(2 * NCH)]
    arrived = {1: rs_left, 3: rs_right}

    def send_single(q):
        cols, far = quarters[q], 4 - near[q]
        tsend[1, :, cols] = partial(far, q).astype(BF16)
        return remote(tsend.at[1, :, cols], arrived[far].at[:, cols], r_send.at[3 * q], r_recv.at[3 * q], ring[far])

    def send_first(q):
        cols = quarters[q]
        tsend[0, :, cols] = partial(2, q).astype(BF16)
        return remote(tsend.at[0, :, cols], rs_in.at[:, cols], r_send.at[3 * q + 1], r_recv.at[3 * q + 1],
                      ring[near[q]])

    def own_parts(q):
        cols = quarters[q]
        tnear[:, cols] = partial(near[q], q)
        tfin[:, cols] = partial(0, q)

    def send_sum(q, first):
        cols = quarters[q]
        with jax.named_scope(f"rs first wait {q}"):
            first.wait_recv()
        tsend[2, :, cols] = (tnear[:, cols] + rs_in[:, cols].astype(F32)).astype(BF16)
        return remote(tsend.at[2, :, cols], arrived[near[q]].at[:, cols], r_send.at[3 * q + 2],
                      r_recv.at[3 * q + 2], ring[near[q]])

    def give_back(i, c):
        for m in range(4):
            part = pl.ds(m * 256, 256)
            send[2 + i, c, part, :] = nn(pack_m[part, :], ys[i, c]).astype(BF16)
        spread(2 + i, c)

    def stack_up(i, c, h, total):
        total = total.astype(BF16)
        for j in range(NSUB):
            ys[i, c, j * ROWS:(j + 1) * ROWS, h * 128:(h + 1) * 128] = total[:, j * 128:(j + 1) * 128]

    with jax.named_scope("gh 1 3 wait"):
        g1.wait_recv()
        g3.wait_recv()
    with jax.named_scope("singles 01"):
        for r in (1, 3, 0):
            grad_group(r)
        singles = [send_single(0), send_single(1)]
    with jax.named_scope("wd on wait"):
        for pair in w_on:
            for copy in pair:
                copy.wait_recv()
    with jax.named_scope("gh 2"):
        g2 = give_grad(2)
    with jax.named_scope("singles 23"):
        singles += [send_single(2), send_single(3)]

    with jax.named_scope("h wait"):
        for copy in (h1, h3, h2):
            copy.wait_recv()
    for c in range(NCH):
        with jax.named_scope(f"out f {c}"):
            for h in range(2):
                total = nn(hf[0], wd[0, :, half(c, h)])
                for r in range(1, RING):
                    total = total + nn(hf[r], wd[r, :, half(c, h)])
                stack_up(0, c, h, total)
            give_back(0, c)

    with jax.named_scope("gh 2 wait"):
        g2.wait_recv()
    with jax.named_scope("firsts"):
        grad_group(2)
        firsts = [send_first(0), send_first(1), send_first(2)]
        own_parts(0)
        own_parts(1)
    summed = [send_sum(0, firsts[0]), send_sum(1, firsts[1])]
    with jax.named_scope("first 3"):
        firsts.append(send_first(3))
        own_parts(2)
        own_parts(3)
    summed += [send_sum(2, firsts[2]), send_sum(3, firsts[3])]

    gate_f = as_column(gates_f[...].astype(BF16).astype(F32))
    gate_b = as_column(gates_b[...].astype(BF16).astype(F32))

    def home(i, c, use):
        def one(j, carry):
            got = nn(get_m[i, pl.ds(pl.multiple_of(j * TOK, TOK), TOK), :], recv[2 + i, c])
            use(col(c, 0, j), got[:, :128])
            use(col(c, 1, j), got[:, 128:])
            return carry
        lax.fori_loop(0, NSUB, one, 0)

    def add_forward(cols, got):
        out_f[:, cols] = (arr[:, cols].astype(F32) + gate_f * got).astype(BF16)

    def home_forward(c):
        with jax.named_scope(f"home f wait {c}"):
            whole(2, c).wait_recv()
        home(0, c, add_forward)

    def finish_sums(c):
        for h in range(2):
            q = 2 * c + h
            cols = quarters[q]
            with jax.named_scope(f"rs final wait {q}"):
                singles[q].wait_recv()
                summed[q].wait_recv()
            stack_up(1, c, h, tfin[:, cols] + rs_left[:, cols].astype(F32) + rs_right[:, cols].astype(F32))
        with jax.named_scope(f"give back b {c}"):
            give_back(1, c)

    kept_wide = kept[...].astype(F32)
    inverse_b = lax.rsqrt(jnp.mean(kept_wide * kept_wide, axis=-1, keepdims=True) + EPS)

    def keep(cols, got):
        gnorm[:, cols] = gate_b * got * gain_ref[:, cols]

    home_forward(0)
    finish_sums(0)
    home_forward(1)
    finish_sums(1)

    for c in range(NCH):
        with jax.named_scope(f"home b wait {c}"):
            whole(3, c).wait_recv()
        home(1, c, keep)
    with jax.named_scope("final"):
        scaled = gnorm[...]
        xhat = kept[...].astype(F32) * inverse_b
        inner = jnp.mean(scaled * xhat, axis=-1, keepdims=True)
        out_b[...] = (ret[...].astype(F32) + inverse_b * (scaled - xhat * inner)).astype(BF16)

    for copy in pending:
        copy.wait_send()
    for i in range(4):
        for c in range(NCH):
            whole(i, c).wait_send()


def on_device(forward_inputs, forward_routes, forward_gates, backward_inputs, backward_cotangent, backward_routes,
              backward_gates, saved_preacts, norm_gain, gate_weight, up_weight, down_weight):
    vmem = pl.BlockSpec(memory_space=pltpu.VMEM)
    hbm = pl.BlockSpec(memory_space=pl.ANY)
    dma = pltpu.SemaphoreType.DMA
    out = jax.ShapeDtypeStruct((TOK, D), BF16)
    scratch = [
        pltpu.VMEM((TOK, D), BF16),
        pltpu.VMEM((TOK, D), BF16),
        pltpu.VMEM((TOK, D), BF16),
        pltpu.VMEM((RING * ROWS, 2 * HID), BF16),
        pltpu.VMEM((D, HID), BF16),
        pltpu.VMEM((D, HID), BF16),
        pltpu.VMEM((RING, HID, D), BF16),
        pltpu.VMEM((2, PACK, NSUB * TOK), BF16),
        pltpu.VMEM((2, NSUB * TOK, PACK), BF16),
        pltpu.VMEM((PACK, NSUB * ROWS), BF16),
        pltpu.VMEM((NSUB * ROWS, PACK), BF16),
        pltpu.VMEM((TOK, D), BF16),
        pltpu.VMEM((4, NCH, PACK, 256), BF16),
        pltpu.VMEM((4, NCH, PACK, 256), BF16),
        pltpu.VMEM((RING, ROWS, D), BF16),
        pltpu.VMEM((ROWS, D), BF16),
        pltpu.VMEM((RING - 1, ROWS, HID), BF16),
        pltpu.VMEM((RING, ROWS, HID), BF16),
        pltpu.VMEM((RING - 1, ROWS, HID), BF16),
        pltpu.VMEM((RING, ROWS, HID), BF16),
        pltpu.VMEM((RING, ROWS, 2 * HID), F32),
        pltpu.VMEM((RING, ROWS, 2 * HID), BF16),
        pltpu.VMEM((3, ROWS, D), BF16),
        pltpu.VMEM((ROWS, D), F32),
        pltpu.VMEM((ROWS, D), F32),
        pltpu.VMEM((ROWS, D), BF16),
        pltpu.VMEM((ROWS, D), BF16),
        pltpu.VMEM((ROWS, D), BF16),
        pltpu.VMEM((2, NCH, NSUB * ROWS, 256), BF16),
        pltpu.VMEM((TOK, D), F32),
        dma((5,)), dma((2,)), dma((2,)), dma((8,)), dma((8,)), dma((8,)), dma((8,)), dma((12,)), dma((12,)),
        dma((3,)), dma((3,)), dma((3,)), dma((3,)), dma((12,)), dma((12,)),
    ]
    call = pl.pallas_call(
        kernel,
        out_shape=(out, out),
        in_specs=[hbm, hbm, hbm, vmem, vmem, vmem, vmem, hbm, vmem, hbm, hbm, hbm],
        out_specs=(vmem, vmem),
        scratch_shapes=scratch,
        compiler_params=pltpu.CompilerParams(collective_id=0, has_side_effects=True,
                                             vmem_limit_bytes=62 * 2 ** 20),
        cost_estimate=pl.CostEstimate(flops=10 ** 10, bytes_accessed=2 * 10 ** 7, transcendentals=10 ** 6),
    )

    def row(values):
        return values.reshape(1, TOK)

    outputs, grads = call(
        forward_inputs[0], backward_cotangent[0], backward_inputs[0], row(forward_routes), row(forward_gates),
        row(backward_routes), row(backward_gates), saved_preacts[0, 0], norm_gain, gate_weight[0], up_weight[0],
        down_weight[0])
    return outputs[None], grads[None]


def solution(mesh):
    tokens = P("pipe", "ep", None)
    in_specs = (tokens,) * 7 + (P("pipe", "ep", None, None), P("pipe", None), P("pipe", None, "ep"),
                                P("pipe", None, "ep"), tokens)
    return jax.shard_map(on_device, mesh=mesh, in_specs=in_specs, out_specs=(tokens, tokens), check_vma=False)
```

```python
import functools
import jax
import jax.numpy as jnp
from jax import lax
from jax.experimental import pallas as pl
from jax.experimental.pallas import tpu as pltpu
from jax.sharding import PartitionSpec as P


RING = 4
NEXP = 16
TOK = 128
D = 3584
HID = 256
CAP = 9
ROWS = NEXP * CAP
NCH = 2
NSUB = 7
HALF = NSUB * 128
BLK = 64
PACK = NEXP * BLK
EPS = 1e-6
MESH = pl.DeviceIdType.MESH
F32 = jnp.float32
BF16 = jnp.bfloat16


def iota(shape, dim):
    return lax.broadcasted_iota(jnp.int32, shape, dim)


def nn(a, b):
    return lax.dot_general(a, b, (((1,), (0,)), ((), ())), preferred_element_type=F32)


def nt(a, b):
    return lax.dot_general(a, b, (((1,), (1,)), ((), ())), preferred_element_type=F32)


def hot(mask):
    return jnp.where(mask, 1.0, 0.0).astype(BF16)


def as_column(row):
    t0, t1 = iota((TOK, TOK), 0), iota((TOK, TOK), 1)
    return jnp.sum(jnp.where(t0 == t1, jnp.broadcast_to(row, (TOK, TOK)), 0.0), axis=1, keepdims=True)


def slot_places(routes):
    t0, t1 = iota((TOK, TOK), 0), iota((TOK, TOK), 1)
    row = routes.astype(F32)
    column = as_column(row)
    same = column == row
    col_before = jnp.sum(jnp.where(same & (t1 < t0), 1.0, 0.0), axis=1, keepdims=True)
    row_before = jnp.sum(jnp.where(same & (t0 < t1), 1.0, 0.0), axis=0, keepdims=True)
    col = column * BLK + col_before
    return (row * BLK + row_before).astype(jnp.int32), col.astype(jnp.int32)


def kernel(fin, cot, bin_hbm, routes_f, gates_f, routes_b, gates_b, saved_hbm, gain_ref, wg_hbm, wu_hbm, wd_hbm,
           out_f, out_b,
           arr, ret, kept, saved, wg, wu, wd, put, get_m, pack_m, unpack_m, normed, send, recv, xs, xb, hs, hf, gs,
           ghb, factor, gj, tsend, tnear, tfin, rs_in, rs_left, rs_right, ys, gnorm,
           loc_sem, p_send, p_recv, w_send, w_recv, d_send, d_recv, a_send, a_recv, h_send, h_recv, g_send, g_recv,
           r_send, r_recv, b_send, b_recv):
    p, ep = lax.axis_index("pipe"), lax.axis_index("ep")
    e, k = ep // RING, ep % RING
    right = (p, e * RING + (k + 1) % RING)
    left = (p, e * RING + (k + 3) % RING)
    opposite = (p, e * RING + (k + 2) % RING)
    after, before = ((p + 1) % 4, ep), ((p + 3) % 4, ep)
    ring = {1: right, 2: opposite, 3: left}
    pending = []

    def remote(src, dst, ssem, rsem, device):
        copy = pltpu.make_async_remote_copy(src_ref=src, dst_ref=dst, send_sem=ssem, recv_sem=rsem, device_id=device,
                                            device_id_type=MESH)
        copy.start()
        pending.append(copy)
        return copy

    loads = [pltpu.make_async_copy(a, b, loc_sem.at[i]) for i, (a, b) in enumerate(
        ((wd_hbm, wd.at[0]), (wg_hbm, wg), (wu_hbm, wu), (saved_hbm, saved), (bin_hbm, kept)))]
    for load in loads:
        load.start()

    barrier = pltpu.get_barrier_semaphore()

    def greet(d, carry):
        pl.semaphore_signal(barrier, inc=1, device_id=(p, (e + d) % NEXP * RING + k), device_id_type=MESH)
        return carry

    lax.fori_loop(1, NEXP, greet, 0)
    for device in (right, left, opposite, after, before):
        pl.semaphore_signal(barrier, inc=1, device_id=device, device_id_type=MESH)
    with jax.named_scope("barrier wait"):
        pl.semaphore_wait(barrier, NEXP - 1 + 5)

    pipe_f = remote(fin, arr, p_send.at[0], p_recv.at[0], after)
    HA, HB = pl.ds(0, HID // 2), pl.ds(HID // 2, HID // 2)
    w_ra = remote(wd_hbm.at[HA], wd.at[3, HA], w_send.at[0], w_recv.at[0], right)
    w_lb = remote(wd_hbm.at[HB], wd.at[1, HB], w_send.at[1], w_recv.at[1], left)
    w_rb = remote(wd_hbm.at[HB], wd.at[3, HB], w_send.at[2], w_recv.at[2], right)
    w_la = remote(wd_hbm.at[HA], wd.at[1, HA], w_send.at[3], w_recv.at[3], left)

    def put_matrix(i, places):
        def one(j, carry):
            put[i, :, pl.ds(pl.multiple_of(j * 128, 128), 128)] = hot(iota((PACK, TOK), 0) == places + j * CAP)
            return carry
        lax.fori_loop(0, NSUB, one, 0)

    def get_matrix(i, places):
        def one(j, carry):
            get_m[i, pl.ds(pl.multiple_of(j * 128, 128), 128), :] = hot(iota((TOK, PACK), 1) == places + j * CAP)
            return carry
        lax.fori_loop(0, NSUB, one, 0)

    def ninth(v):
        return (v * 57) >> 9

    def unpack_matrix():
        def one(j, carry):
            r = iota((ROWS, PACK), 0)
            unpack_m[pl.ds(pl.multiple_of(j * ROWS, 16), ROWS), :] = hot(
                iota((ROWS, PACK), 1) == ninth(r) * (BLK - CAP) + r + j * CAP)
            return carry
        lax.fori_loop(0, NSUB, one, 0)

    def pack_matrix():
        for j in range(NSUB):
            r = iota((PACK, ROWS), 1)
            pack_m[:, j * ROWS:(j + 1) * ROWS] = hot(
                iota((PACK, ROWS), 0) == ninth(r) * (BLK - CAP) + r + j * CAP)

    def spread(i, c):
        s = 2 * i + c

        def one(d, carry):
            to = (e + d) % NEXP
            pltpu.make_async_remote_copy(
                src_ref=send.at[i, c, pl.ds(pl.multiple_of(to * BLK, BLK), BLK)],
                dst_ref=recv.at[i, c, pl.ds(pl.multiple_of(e * BLK, BLK), BLK)],
                send_sem=d_send.at[s], recv_sem=d_recv.at[s],
                device_id=(p, to * RING + k), device_id_type=MESH).start()
            return carry
        lax.fori_loop(1, NEXP, one, 0)
        own = pl.ds(pl.multiple_of(e * BLK, BLK), BLK)
        recv[i, c, own, :] = send[i, c, own, :]

    def whole(i, c):
        part = pl.ds(0, PACK - BLK)
        return pltpu.make_async_remote_copy(
            src_ref=send.at[i, c, part], dst_ref=recv.at[i, c, part],
            send_sem=d_send.at[2 * i + c], recv_sem=d_recv.at[2 * i + c], device_id=right, device_id_type=MESH)

    def half(c, h):
        return pl.ds((2 * c + h) * HALF, HALF)

    def col(c, h, j):
        return pl.ds(pl.multiple_of((2 * c + h) * HALF + j * 128, 128), 128)

    def dispatch(i, values):
        for c in range(NCH):
            stack = jnp.concatenate([
                jnp.concatenate([values[:, (2 * c + h) * HALF + j * 128:(2 * c + h) * HALF + (j + 1) * 128]
                                 for h in range(2)], axis=1) for j in range(NSUB)], axis=0)
            for m in range(4):
                part = pl.ds(m * 256, 256)
                send[i, c, part, :] = nn(put[i, part, :], stack).astype(BF16)
            spread(i, c)

    def unpack(i, c, target):
        def one(j, carry):
            got = nn(unpack_m[pl.ds(pl.multiple_of(j * ROWS, 16), ROWS), :], recv[i, c]).astype(BF16)
            target[:, col(c, 0, j)] = got[:, :128]
            target[:, col(c, 1, j)] = got[:, 128:]
            return carry
        lax.fori_loop(0, NSUB, one, 0)

    def saved_factors(r):
        group = (k + r) % RING
        q = iota((ROWS, NEXP * RING * CAP), 0)
        take = hot(iota((ROWS, NEXP * RING * CAP), 1) == ninth(q) * (RING - 1) * CAP + q + group * CAP)
        pre = nn(take, saved[...])
        gate, up = pre[:, :HID], pre[:, HID:]
        sigma = 1.0 / (1.0 + jnp.exp(-gate))
        factor[r, :, :HID] = up * sigma * (1.0 + gate * (1.0 - sigma))
        factor[r, :, HID:] = gate * sigma

    rows_f, cols_f = slot_places(routes_f[...])
    rows_b, cols_b = slot_places(routes_b[...])
    put_matrix(0, rows_f)

    with jax.named_scope("pipe f wait"):
        pipe_f.wait_recv()
    pipe_b = remote(cot, ret, p_send.at[1], p_recv.at[1], before)
    wide = arr[...].astype(F32)
    inverse = lax.rsqrt(jnp.mean(wide * wide, axis=-1, keepdims=True) + EPS)
    normed[...] = (wide * inverse * gain_ref[...]).astype(BF16)
    with jax.named_scope("dispatch f"):
        dispatch(0, normed)

    put_matrix(1, rows_b)
    unpack_matrix()
    for load in loads:
        load.wait()
    with jax.named_scope("saved factors"):
        for r in range(RING):
            saved_factors(r)

    with jax.named_scope("pipe b wait"):
        pipe_b.wait_recv()
    with jax.named_scope("dispatch b"):
        dispatch(1, ret)

    with jax.named_scope("matrices"):
        pack_matrix()
        get_matrix(0, cols_f)
        get_matrix(1, cols_b)

    def gather(c):
        with jax.named_scope(f"f disp wait {c}"):
            whole(0, c).wait_recv()
        unpack(0, c, xs.at[0])
        A, B = half(c, 0), half(c, 1)
        o = 6 * c
        x_ra = remote(xs.at[0, :, A], xs.at[3, :, A], a_send.at[o], a_recv.at[o], right)
        x_lb = remote(xs.at[0, :, B], xs.at[1, :, B], a_send.at[o + 1], a_recv.at[o + 1], left)
        x_rb = remote(xs.at[0, :, B], xs.at[3, :, B], a_send.at[o + 2], a_recv.at[o + 2], right)
        x_la = remote(xs.at[0, :, A], xs.at[1, :, A], a_send.at[o + 3], a_recv.at[o + 3], left)
        return x_ra, x_lb, x_rb, x_la

    def gather_on(c, x_ra, x_lb):
        A, B = half(c, 0), half(c, 1)
        o = 6 * c
        with jax.named_scope(f"x ra wait {c}"):
            x_ra.wait_recv()
        x_f = remote(xs.at[3, :, A], xs.at[2, :, A], a_send.at[o + 4], a_recv.at[o + 4], right)
        with jax.named_scope(f"x lb wait {c}"):
            x_lb.wait_recv()
        x_g = remote(xs.at[1, :, B], xs.at[2, :, B], a_send.at[o + 5], a_recv.at[o + 5], left)
        return x_f, x_g

    def weights_on(part):
        cols = pl.ds(part * 2 * HALF, 2 * HALF)
        o = 4 + 2 * part
        return (remote(wd.at[3, HA, cols], wd.at[2, HA, cols], w_send.at[o], w_recv.at[o], right),
                remote(wd.at[1, HB, cols], wd.at[2, HB, cols], w_send.at[o + 1], w_recv.at[o + 1], left))

    def grad_hidden(r):
        return nt(xb[...], wd[r]).astype(BF16)

    def give_grad(r):
        gs[r - 1] = grad_hidden(r)
        return remote(gs.at[r - 1], ghb.at[RING - r], g_send.at[r - 1], g_recv.at[r - 1], ring[r])

    def hidden(r):
        rows = xs[r]
        pre_gate = nn(rows, wg[...])
        pre_up = nn(rows, wu[...])
        return (pre_gate / (1.0 + jnp.exp(-pre_gate)) * pre_up).astype(BF16)

    def give_hidden(r):
        hs[r - 1] = hidden(r)
        return remote(hs.at[r - 1], hf.at[RING - r], h_send.at[r - 1], h_recv.at[r - 1], ring[r])

    gathers = [gather(c) for c in range(NCH)]
    x_fwd = [gather_on(0, *gathers[0][:2])]
    with jax.named_scope("hidden 0"):
        hf[0] = hidden(0)

    with jax.named_scope("b disp wait 0"):
        whole(1, 0).wait_recv()
    unpack(1, 0, xb)
    x_fwd.append(gather_on(1, *gathers[1][:2]))
    with jax.named_scope("wd wait"):
        w_ra.wait_recv()
        w_lb.wait_recv()
    w_on = [weights_on(0)]
    with jax.named_scope("b disp wait 1"):
        whole(1, 1).wait_recv()
    unpack(1, 1, xb)

    with jax.named_scope("wd rest wait"):
        w_rb.wait_recv()
        w_la.wait_recv()
    with jax.named_scope("gh 3 1 0"):
        g3 = give_grad(3)
        g1 = give_grad(1)
        ghb[0] = grad_hidden(0)
    with jax.named_scope("x rb la wait"):
        for x_ra, x_lb, x_rb, x_la in gathers:
            x_rb.wait_recv()
            x_la.wait_recv()
    with jax.named_scope("hidden 1 3"):
        h1 = give_hidden(1)
        h3 = give_hidden(3)
    with jax.named_scope("x fwd wait"):
        for x_f, x_g in x_fwd:
            x_f.wait_recv()
            x_g.wait_recv()
    with jax.named_scope("hidden 2"):
        h2 = give_hidden(2)
    w_on.append(weights_on(1))

    def grad_group(r):
        grad = ghb[r].astype(F32)
        gj[r, :, :HID] = (grad * factor[r, :, :HID]).astype(BF16)
        gj[r, :, HID:] = (grad * factor[r, :, HID:]).astype(BF16)

    def partial(r, q, rows):
        cols = pl.ds(q * HALF, HALF)
        return nt(gj[r, rows, :HID], wg[cols, :]) + nt(gj[r, rows, HID:], wu[cols, :])

    quarters = [pl.ds(q * HALF, HALF) for q in range(2 * NCH)]
    cut = [64, 80, 64, 80]
    upper = [pl.ds(0, n) for n in cut]
    lower = [pl.ds(n, ROWS - n) for n in cut]

    def ring_copy(i, q, kind, rows, target, device):
        cols = quarters[q]
        n = 6 * q + 2 * kind + i
        return remote(tsend.at[kind, rows, cols], target.at[rows, cols], r_send.at[n], r_recv.at[n], device)

    def send_single(q):
        cols, a, b = quarters[q], upper[q], lower[q]
        tsend[1, a, cols] = partial(3, q, a).astype(BF16)
        one = ring_copy(0, q, 1, a, rs_right, left)
        tsend[1, b, cols] = partial(1, q, b).astype(BF16)
        return one, ring_copy(1, q, 1, b, rs_left, right)

    def send_first(q):
        cols, a, b = quarters[q], upper[q], lower[q]
        tsend[0, :, cols] = partial(2, q, pl.ds(0, ROWS)).astype(BF16)
        return ring_copy(0, q, 0, a, rs_in, right), ring_copy(1, q, 0, b, rs_in, left)

    def own_parts(q):
        cols, a, b = quarters[q], upper[q], lower[q]
        tnear[a, cols] = partial(1, q, a)
        tnear[b, cols] = partial(3, q, b)
        tfin[:, cols] = partial(0, q, pl.ds(0, ROWS))

    def send_sum(q, first):
        cols, a, b = quarters[q], upper[q], lower[q]
        with jax.named_scope(f"rs first wait {q}"):
            first[0].wait_recv()
        tsend[2, a, cols] = (tnear[a, cols] + rs_in[a, cols].astype(F32)).astype(BF16)
        one = ring_copy(0, q, 2, a, rs_left, right)
        with jax.named_scope(f"rs first wait {q} b"):
            first[1].wait_recv()
        tsend[2, b, cols] = (tnear[b, cols] + rs_in[b, cols].astype(F32)).astype(BF16)
        return one, ring_copy(1, q, 2, b, rs_right, left)

    def give_back(i, c):
        for m in range(4):
            part = pl.ds(m * 256, 256)
            send[2 + i, c, part, :] = nn(pack_m[part, :], ys[i, c]).astype(BF16)
        spread(2 + i, c)

    def stack_up(i, c, h, total):
        total = total.astype(BF16)
        for j in range(NSUB):
            ys[i, c, j * ROWS:(j + 1) * ROWS, h * 128:(h + 1) * 128] = total[:, j * 128:(j + 1) * 128]

    def give_back_quarter(q):
        c, lanes = q // 2, pl.ds(q % 2 * 128, 128)
        for m in range(4):
            part = pl.ds(m * 256, 256)
            send[3, c, part, lanes] = nn(pack_m[part, :], ys[1, c, :, lanes]).astype(BF16)

        def one(d, carry):
            to = (e + d) % NEXP
            pltpu.make_async_remote_copy(
                src_ref=send.at[3, c, pl.ds(pl.multiple_of(to * BLK, BLK), BLK), lanes],
                dst_ref=recv.at[3, c, pl.ds(pl.multiple_of(e * BLK, BLK), BLK), lanes],
                send_sem=b_send.at[q], recv_sem=b_recv.at[q],
                device_id=(p, to * RING + k), device_id_type=MESH).start()
            return carry
        lax.fori_loop(1, NEXP, one, 0)
        own = pl.ds(pl.multiple_of(e * BLK, BLK), BLK)
        recv[3, c, own, lanes] = send[3, c, own, lanes]

    def whole_quarter(q):
        c, lanes = q // 2, pl.ds(q % 2 * 128, 128)
        part = pl.ds(0, PACK - BLK)
        return pltpu.make_async_remote_copy(
            src_ref=send.at[3, c, part, lanes], dst_ref=recv.at[3, c, part, lanes],
            send_sem=b_send.at[q], recv_sem=b_recv.at[q], device_id=right, device_id_type=MESH)

    def forward_out(c):
        with jax.named_scope(f"out f {c}"):
            for h in range(2):
                total = nn(hf[0], wd[0, :, half(c, h)])
                for r in range(1, RING):
                    total = total + nn(hf[r], wd[r, :, half(c, h)])
                stack_up(0, c, h, total)
            give_back(0, c)

    with jax.named_scope("gh 1 3 wait"):
        g1.wait_recv()
        g3.wait_recv()
    with jax.named_scope("singles 0"):
        for r in (1, 3, 0):
            grad_group(r)
        singles = [send_single(0)]
    with jax.named_scope("h wait"):
        for copy in (h1, h3, h2):
            copy.wait_recv()
    with jax.named_scope("wd on wait 0"):
        for copy in w_on[0]:
            copy.wait_recv()
    forward_out(0)
    singles.append(send_single(1))
    with jax.named_scope("wd on wait 1"):
        for copy in w_on[1]:
            copy.wait_recv()
    with jax.named_scope("gh 2"):
        g2 = give_grad(2)
    with jax.named_scope("singles 23"):
        singles += [send_single(2), send_single(3)]
    forward_out(1)

    gate_f = as_column(gates_f[...].astype(BF16).astype(F32))
    gate_b = as_column(gates_b[...].astype(BF16).astype(F32))
    kept_wide = kept[...].astype(F32)
    inverse_b = lax.rsqrt(jnp.mean(kept_wide * kept_wide, axis=-1, keepdims=True) + EPS)

    def home_forward(c):
        with jax.named_scope(f"home f wait {c}"):
            whole(2, c).wait_recv()

        def one(j, carry):
            got = nn(get_m[0, pl.ds(pl.multiple_of(j * TOK, TOK), TOK), :], recv[2, c])
            for h in range(2):
                cols = col(c, h, j)
                out_f[:, cols] = (arr[:, cols].astype(F32) + gate_f * got[:, h * 128:(h + 1) * 128]).astype(BF16)
            return carry
        lax.fori_loop(0, NSUB, one, 0)

    def home_backward(q):
        with jax.named_scope(f"home b wait {q}"):
            whole_quarter(q).wait_recv()
        c, h = q // 2, q % 2

        def one(j, carry):
            got = nn(get_m[1, pl.ds(pl.multiple_of(j * TOK, TOK), TOK), :], recv[3, c, :, h * 128:(h + 1) * 128])
            cols = col(c, h, j)
            gnorm[:, cols] = gate_b * got * gain_ref[:, cols]
            return carry
        lax.fori_loop(0, NSUB, one, 0)

    def finish_sum(q):
        cols = quarters[q]
        with jax.named_scope(f"rs final wait {q}"):
            for copy in singles[q] + summed[q]:
                copy.wait_recv()
        stack_up(1, q // 2, q % 2, tfin[:, cols] + rs_left[:, cols].astype(F32) + rs_right[:, cols].astype(F32))
        with jax.named_scope(f"give back b {q}"):
            give_back_quarter(q)

    with jax.named_scope("gh 2 wait"):
        g2.wait_recv()
    summed = []
    with jax.named_scope("firsts"):
        grad_group(2)
        firsts = [send_first(0), send_first(1)]
        own_parts(0)
        own_parts(1)
    for q in range(2 * NCH):
        summed.append(send_sum(q, firsts[q]))
        if q + 2 < 2 * NCH:
            firsts.append(send_first(q + 2))
            own_parts(q + 2)
        if q > 0:
            finish_sum(q - 1)
        if q > 1:
            home_forward(q - 2)
    finish_sum(2 * NCH - 1)

    for q in range(2 * NCH):
        home_backward(q)
    with jax.named_scope("final"):
        scaled = gnorm[...]
        xhat = kept[...].astype(F32) * inverse_b
        inner = jnp.mean(scaled * xhat, axis=-1, keepdims=True)
        out_b[...] = (ret[...].astype(F32) + inverse_b * (scaled - xhat * inner)).astype(BF16)

    for copy in pending:
        copy.wait_send()
    for i in range(3):
        for c in range(NCH):
            whole(i, c).wait_send()
    for q in range(2 * NCH):
        whole_quarter(q).wait_send()


def on_device(forward_inputs, forward_routes, forward_gates, backward_inputs, backward_cotangent, backward_routes,
              backward_gates, saved_preacts, norm_gain, gate_weight, up_weight, down_weight):
    vmem = pl.BlockSpec(memory_space=pltpu.VMEM)
    hbm = pl.BlockSpec(memory_space=pl.ANY)
    dma = pltpu.SemaphoreType.DMA
    out = jax.ShapeDtypeStruct((TOK, D), BF16)
    scratch = [
        pltpu.VMEM((TOK, D), BF16),
        pltpu.VMEM((TOK, D), BF16),
        pltpu.VMEM((TOK, D), BF16),
        pltpu.VMEM((RING * ROWS, 2 * HID), BF16),
        pltpu.VMEM((D, HID), BF16),
        pltpu.VMEM((D, HID), BF16),
        pltpu.VMEM((RING, HID, D), BF16),
        pltpu.VMEM((2, PACK, NSUB * TOK), BF16),
        pltpu.VMEM((2, NSUB * TOK, PACK), BF16),
        pltpu.VMEM((PACK, NSUB * ROWS), BF16),
        pltpu.VMEM((NSUB * ROWS, PACK), BF16),
        pltpu.VMEM((TOK, D), BF16),
        pltpu.VMEM((4, NCH, PACK, 256), BF16),
        pltpu.VMEM((4, NCH, PACK, 256), BF16),
        pltpu.VMEM((RING, ROWS, D), BF16),
        pltpu.VMEM((ROWS, D), BF16),
        pltpu.VMEM((RING - 1, ROWS, HID), BF16),
        pltpu.VMEM((RING, ROWS, HID), BF16),
        pltpu.VMEM((RING - 1, ROWS, HID), BF16),
        pltpu.VMEM((RING, ROWS, HID), BF16),
        pltpu.VMEM((RING, ROWS, 2 * HID), F32),
        pltpu.VMEM((RING, ROWS, 2 * HID), BF16),
        pltpu.VMEM((3, ROWS, D), BF16),
        pltpu.VMEM((ROWS, D), F32),
        pltpu.VMEM((ROWS, D), F32),
        pltpu.VMEM((ROWS, D), BF16),
        pltpu.VMEM((ROWS, D), BF16),
        pltpu.VMEM((ROWS, D), BF16),
        pltpu.VMEM((2, NCH, NSUB * ROWS, 256), BF16),
        pltpu.VMEM((TOK, D), F32),
        dma((5,)), dma((2,)), dma((2,)), dma((8,)), dma((8,)), dma((8,)), dma((8,)), dma((12,)), dma((12,)),
        dma((3,)), dma((3,)), dma((3,)), dma((3,)), dma((24,)), dma((24,)), dma((4,)), dma((4,)),
    ]
    call = pl.pallas_call(
        kernel,
        out_shape=(out, out),
        in_specs=[hbm, hbm, hbm, vmem, vmem, vmem, vmem, hbm, vmem, hbm, hbm, hbm],
        out_specs=(vmem, vmem),
        scratch_shapes=scratch,
        compiler_params=pltpu.CompilerParams(collective_id=0, has_side_effects=True,
                                             vmem_limit_bytes=62 * 2 ** 20),
        cost_estimate=pl.CostEstimate(flops=10 ** 10, bytes_accessed=2 * 10 ** 7, transcendentals=10 ** 6),
    )

    def row(values):
        return values.reshape(1, TOK)

    outputs, grads = call(
        forward_inputs[0], backward_cotangent[0], backward_inputs[0], row(forward_routes), row(forward_gates),
        row(backward_routes), row(backward_gates), saved_preacts[0, 0], norm_gain, gate_weight[0], up_weight[0],
        down_weight[0])
    return outputs[None], grads[None]


def solution(mesh):
    tokens = P("pipe", "ep", None)
    in_specs = (tokens,) * 7 + (P("pipe", "ep", None, None), P("pipe", None), P("pipe", None, "ep"),
                                P("pipe", None, "ep"), tokens)
    return jax.shard_map(on_device, mesh=mesh, in_specs=in_specs, out_specs=(tokens, tokens), check_vma=False)
```

```python
import functools
import jax
import jax.numpy as jnp
from jax import lax
from jax.experimental import pallas as pl
from jax.experimental.pallas import tpu as pltpu
from jax.sharding import PartitionSpec as P


RING = 4
NEXP = 16
TOK = 128
D = 3584
HID = 256
CAP = 9
ROWS = NEXP * CAP
NCH = 2
NSUB = 7
HALF = NSUB * 128
BLK = 64
PACK = NEXP * BLK
EPS = 1e-6
MESH = pl.DeviceIdType.MESH
F32 = jnp.float32
BF16 = jnp.bfloat16


def iota(shape, dim):
    return lax.broadcasted_iota(jnp.int32, shape, dim)


def nn(a, b):
    return lax.dot_general(a, b, (((1,), (0,)), ((), ())), preferred_element_type=F32)


def nt(a, b):
    return lax.dot_general(a, b, (((1,), (1,)), ((), ())), preferred_element_type=F32)


def hot(mask):
    return jnp.where(mask, 1.0, 0.0).astype(BF16)


def as_column(row):
    t0, t1 = iota((TOK, TOK), 0), iota((TOK, TOK), 1)
    return jnp.sum(jnp.where(t0 == t1, jnp.broadcast_to(row, (TOK, TOK)), 0.0), axis=1, keepdims=True)


def slot_places(routes):
    t0, t1 = iota((TOK, TOK), 0), iota((TOK, TOK), 1)
    row = routes.astype(F32)
    column = as_column(row)
    same = column == row
    col_before = jnp.sum(jnp.where(same & (t1 < t0), 1.0, 0.0), axis=1, keepdims=True)
    row_before = jnp.sum(jnp.where(same & (t0 < t1), 1.0, 0.0), axis=0, keepdims=True)
    col = column * BLK + col_before
    return (row * BLK + row_before).astype(jnp.int32), col.astype(jnp.int32)


def kernel(fin, cot, bin_hbm, routes_f, gates_f, routes_b, gates_b, saved_hbm, gain_ref, wg_hbm, wu_hbm, wd_hbm,
           out_f, out_b,
           arr, ret, kept, saved, wg, wu, wd, put, get_m, pack_m, unpack_m, next_routes, next_gain, normed, send, recv, xs, xb, xbn, hk, hs, hp,
           hn, fs, fr, gsn, gpn, gsp, ghb, factor, gj, tsend, tnear, tfin, rs_in, rs_p, rs_n, ys, gnorm,
           loc_sem, p_send, p_recv, w_send, w_recv, d_send, d_recv, a_send, a_recv, h_send, h_recv, g_send, g_recv,
           r_send, r_recv, b_send, b_recv):
    p, ep = lax.axis_index("pipe"), lax.axis_index("ep")
    e, k = ep // RING, ep % RING
    groups = (k, k + 1 - 2 * (k % 2), RING - 1 - k, (k + 2) % RING)
    pair, next_pair = (p, e * RING + groups[1]), (p, e * RING + groups[2])
    after, before = ((p + 1) % 4, ep), ((p + 3) % 4, ep)
    pending = []

    def remote(src, dst, ssem, rsem, device):
        copy = pltpu.make_async_remote_copy(src_ref=src, dst_ref=dst, send_sem=ssem, recv_sem=rsem, device_id=device,
                                            device_id_type=MESH)
        copy.start()
        pending.append(copy)
        return copy

    loads = [pltpu.make_async_copy(a, b, loc_sem.at[i]) for i, (a, b) in enumerate(
        ((fin, normed), (wd_hbm, wd.at[0]), (wg_hbm, wg), (wu_hbm, wu), (saved_hbm, saved), (bin_hbm, kept)))]
    for load in loads:
        load.start()

    barrier = pltpu.get_barrier_semaphore()

    def greet(d, carry):
        pl.semaphore_signal(barrier, inc=1, device_id=(p, (e + d) % NEXP * RING + k), device_id_type=MESH)
        return carry

    def greet_before(d, carry):
        pl.semaphore_signal(barrier, inc=1, device_id=((p + 3) % 4, (e + d) % NEXP * RING + k), device_id_type=MESH)
        return carry

    lax.fori_loop(1, NEXP, greet, 0)
    lax.fori_loop(0, NEXP, greet_before, 0)
    for device in (pair, next_pair, after):
        pl.semaphore_signal(barrier, inc=1, device_id=device, device_id_type=MESH)
    with jax.named_scope("barrier wait"):
        pl.semaphore_wait(barrier, NEXP - 1 + NEXP + 3)

    to_routes = remote(routes_f, next_routes, p_send.at[2], p_recv.at[2], before)
    to_gain = remote(gain_ref, next_gain, p_send.at[3], p_recv.at[3], before)
    pipe_b = remote(cot, ret, p_send.at[1], p_recv.at[1], before)
    HA, HB = pl.ds(0, HID // 2), pl.ds(HID // 2, HID // 2)
    F1, F2 = pl.ds(0, 2 * HALF), pl.ds(2 * HALF, 2 * HALF)
    w_pb = remote(wd_hbm.at[HB, F1], wd.at[1, HB, F1], w_send.at[0], w_recv.at[0], pair)
    w_na = remote(wd_hbm.at[HA, F1], wd.at[2, HA, F1], w_send.at[1], w_recv.at[1], next_pair)
    w_pa = remote(wd_hbm.at[HA, F1], wd.at[1, HA, F1], w_send.at[2], w_recv.at[2], pair)
    w_nb = remote(wd_hbm.at[HB, F1], wd.at[2, HB, F1], w_send.at[3], w_recv.at[3], next_pair)

    def put_matrix(i, places):
        def one(j, carry):
            put[i, :, pl.ds(pl.multiple_of(j * 128, 128), 128)] = hot(iota((PACK, TOK), 0) == places + j * CAP)
            return carry
        lax.fori_loop(0, NSUB, one, 0)

    def get_matrix(i, places):
        def one(j, carry):
            get_m[i, pl.ds(pl.multiple_of(j * 128, 128), 128), :] = hot(iota((TOK, PACK), 1) == places + j * CAP)
            return carry
        lax.fori_loop(0, NSUB, one, 0)

    def ninth(v):
        return (v * 57) >> 9

    def unpack_matrix():
        def one(j, carry):
            r = iota((ROWS, PACK), 0)
            unpack_m[pl.ds(pl.multiple_of(j * ROWS, 16), ROWS), :] = hot(
                iota((ROWS, PACK), 1) == ninth(r) * (BLK - CAP) + r + j * CAP)
            return carry
        lax.fori_loop(0, NSUB, one, 0)

    def pack_matrix():
        for j in range(NSUB):
            r = iota((PACK, ROWS), 1)
            pack_m[:, j * ROWS:(j + 1) * ROWS] = hot(
                iota((PACK, ROWS), 0) == ninth(r) * (BLK - CAP) + r + j * CAP)

    def place(d):
        odd = d % 2
        return (e + odd * ((d + 1) // 2) + (1 - odd) * (NEXP - d // 2)) % NEXP

    def spread(i, c):
        s = 2 * i + c
        section = (p + 1) % 4 if i == 0 else p

        own = pl.ds(pl.multiple_of(e * BLK, BLK), BLK)

        def block(to):
            pltpu.make_async_remote_copy(
                src_ref=send.at[i, c, pl.ds(pl.multiple_of(to * BLK, BLK), BLK)], dst_ref=recv.at[i, c, own],
                send_sem=d_send.at[s], recv_sem=d_recv.at[s],
                device_id=(section, to * RING + k), device_id_type=MESH).start()

        def one(d, carry):
            block(place(d))
            return carry
        lax.fori_loop(1, NEXP, one, 0)
        if i > 0:
            recv[i, c, own, :] = send[i, c, own, :]
        else:
            block(e)

    def whole(i, c):
        part = pl.ds(0, PACK if i == 0 else PACK - BLK)
        return pltpu.make_async_remote_copy(
            src_ref=send.at[i, c, part], dst_ref=recv.at[i, c, part],
            send_sem=d_send.at[2 * i + c], recv_sem=d_recv.at[2 * i + c], device_id=pair, device_id_type=MESH)

    def half(c, h):
        return pl.ds((2 * c + h) * HALF, HALF)

    def col(c, h, j):
        return pl.ds(pl.multiple_of((2 * c + h) * HALF + j * 128, 128), 128)

    def dispatch(i, values, order):
        for c in order:
            stack = jnp.concatenate([
                jnp.concatenate([values[:, (2 * c + h) * HALF + j * 128:(2 * c + h) * HALF + (j + 1) * 128]
                                 for h in range(2)], axis=1) for j in range(NSUB)], axis=0)
            for m in range(4):
                part = pl.ds(m * 256, 256)
                send[i, c, part, :] = nn(put[i, part, :], stack).astype(BF16)
            spread(i, c)

    def unpack(i, c, target):
        def one(j, carry):
            got = nn(unpack_m[pl.ds(pl.multiple_of(j * ROWS, 16), ROWS), :], recv[i, c]).astype(BF16)
            target[:, col(c, 0, j)] = got[:, :128]
            target[:, col(c, 1, j)] = got[:, 128:]
            return carry
        lax.fori_loop(0, NSUB, one, 0)

    def saved_factors(r):
        group = groups[r]
        q = iota((ROWS, NEXP * RING * CAP), 0)
        take = hot(iota((ROWS, NEXP * RING * CAP), 1) == ninth(q) * (RING - 1) * CAP + q + group * CAP)
        pre = nn(take, saved[...])
        gate, up = pre[:, :HID], pre[:, HID:]
        sigma = 1.0 / (1.0 + jnp.exp(-gate))
        factor[r, :, :HID] = up * sigma * (1.0 + gate * (1.0 - sigma))
        factor[r, :, HID:] = gate * sigma

    loads[0].wait()
    wide = normed[...].astype(F32)
    inverse = lax.rsqrt(jnp.mean(wide * wide, axis=-1, keepdims=True) + EPS)
    with jax.named_scope("routes wait"):
        to_routes.wait_recv()
        to_gain.wait_recv()
    put_matrix(0, slot_places(next_routes[...])[0])
    normed[...] = (wide * inverse * next_gain[...]).astype(BF16)
    with jax.named_scope("dispatch f"):
        dispatch(0, normed, (0, 1))

    cols_f = slot_places(routes_f[...])[1]
    rows_b, cols_b = slot_places(routes_b[...])
    put_matrix(1, rows_b)
    unpack_matrix()
    for load in loads[1:]:
        load.wait()
    with jax.named_scope("saved factors"):
        for r in range(RING):
            saved_factors(r)

    with jax.named_scope("wd fwd wait"):
        w_na.wait_recv()
    w_pf = remote(wd.at[2, HA, F1], wd.at[3, HA, F1], w_send.at[4], w_recv.at[4], pair)
    w_pb.wait_recv()
    w_nf = remote(wd.at[1, HB, F1], wd.at[3, HB, F1], w_send.at[5], w_recv.at[5], next_pair)

    def gather(c):
        with jax.named_scope(f"f disp wait {c}"):
            whole(0, c).wait_recv()
        unpack(0, c, xs.at[0])
        A, B = half(c, 0), half(c, 1)
        o = 6 * c
        x_pb = remote(xs.at[0, :, B], xs.at[1, :, B], a_send.at[o], a_recv.at[o], pair)
        x_na = remote(xs.at[0, :, A], xs.at[2, :, A], a_send.at[o + 1], a_recv.at[o + 1], next_pair)
        x_pa = remote(xs.at[0, :, A], xs.at[1, :, A], a_send.at[o + 2], a_recv.at[o + 2], pair)
        x_nb = remote(xs.at[0, :, B], xs.at[2, :, B], a_send.at[o + 3], a_recv.at[o + 3], next_pair)
        return x_pb, x_na, x_pa, x_nb

    def on_to_pair(c):
        A, o = half(c, 0), 6 * c + 4
        return remote(xs.at[2, :, A], xs.at[3, :, A], a_send.at[o], a_recv.at[o], pair)

    def on_to_next(c):
        B, o = half(c, 1), 6 * c + 5
        return remote(xs.at[1, :, B], xs.at[3, :, B], a_send.at[o], a_recv.at[o], next_pair)

    def hidden(r):
        rows = xs[r]
        pre_gate = nn(rows, wg[...])
        pre_up = nn(rows, wu[...])
        return (pre_gate / (1.0 + jnp.exp(-pre_gate)) * pre_up).astype(BF16)

    gathers = [gather(0)]

    with jax.named_scope("pipe b wait"):
        pipe_b.wait_recv()
    with jax.named_scope("dispatch b"):
        dispatch(1, ret, (1, 0))
    pipe_f = remote(fin, arr, p_send.at[0], p_recv.at[0], after)

    gathers.append(gather(1))
    with jax.named_scope("hidden 0"):
        hk[0] = hidden(0)

    with jax.named_scope("matrices"):
        pack_matrix()
        get_matrix(0, cols_f)
        get_matrix(1, cols_b)

    x_on = []
    for c in range(NCH):
        with jax.named_scope(f"x na pb wait {c}"):
            gathers[c][1].wait_recv()
            x_on.append(on_to_pair(c))
            gathers[c][0].wait_recv()
            x_on.append(on_to_next(c))

    def exchange_f2(i, rows):
        cols = (rows, F2)
        return remote(wd_hbm.at[cols], wd.at[(1,) + cols], w_send.at[6 + i], w_recv.at[6 + i], pair)

    with jax.named_scope("b disp wait 1"):
        whole(1, 1).wait_recv()
    unpack(1, 1, xb)
    b_rows = remote(xb.at[:, F2], xbn, g_send.at[0], g_recv.at[0], next_pair)
    w_f2 = [exchange_f2(0, HA)]
    with jax.named_scope("b disp wait 0"):
        whole(1, 0).wait_recv()
    unpack(1, 0, xb)
    with jax.named_scope("wd F1 wait"):
        for copy in (w_pa, w_nb, w_pf, w_nf):
            copy.wait_recv()
    with jax.named_scope("gh F1"):
        for r in (2, 3):
            gsn[:, (r - 2) * HID:(r - 1) * HID] = nt(xb[:, F1], wd[r, :, F1]).astype(BF16)
        b_part = remote(gsn, gpn, g_send.at[1], g_recv.at[1], next_pair)
        ghb[0] = nt(xb[...], wd[0]).astype(BF16)

    with jax.named_scope("x rest wait"):
        for c in range(NCH):
            gathers[c][2].wait_recv()
            gathers[c][3].wait_recv()
    with jax.named_scope("hidden 2 1"):
        hk[1] = hidden(2)
        h_n0 = remote(hk.at[1], hn.at[0], h_send.at[0], h_recv.at[0], next_pair)
        hs[0] = hidden(1)
        h_p0 = remote(hs.at[0], hp.at[0], h_send.at[1], h_recv.at[1], pair)
    with jax.named_scope("x on wait"):
        for copy in x_on:
            copy.wait_recv()
    with jax.named_scope("hidden 3"):
        hs[1] = hidden(3)
        h_p1 = remote(hs.at[1], hp.at[1], h_send.at[2], h_recv.at[2], pair)
    w_f2.append(exchange_f2(1, HB))

    def grad_group(r):
        grad = ghb[r].astype(F32)
        gj[r, :, :HID] = (grad * factor[r, :, :HID]).astype(BF16)
        gj[r, :, HID:] = (grad * factor[r, :, HID:]).astype(BF16)

    def partial(r, q, rows):
        cols = pl.ds(q * HALF, HALF)
        return nt(gj[r, rows, :HID], wg[cols, :]) + nt(gj[r, rows, HID:], wu[cols, :])

    quarters = [pl.ds(q * HALF, HALF) for q in range(2 * NCH)]
    cut = [80, 64, 80, 64]
    upper = [pl.ds(0, n) for n in cut]
    lower = [pl.ds(n, ROWS - n) for n in cut]

    def ring_copy(i, q, kind, rows, target, device):
        cols = quarters[q]
        n = 6 * q + 2 * kind + i
        return remote(tsend.at[kind, rows, cols], target.at[rows, cols], r_send.at[n], r_recv.at[n], device)

    def send_single_pair(q):
        cols, a = quarters[q], upper[q]
        tsend[1, a, cols] = partial(1, q, a).astype(BF16)
        return ring_copy(0, q, 1, a, rs_p, pair)

    def send_single_next(q):
        cols, b = quarters[q], lower[q]
        tsend[1, b, cols] = partial(2, q, b).astype(BF16)
        return ring_copy(1, q, 1, b, rs_n, next_pair)

    def send_first(q):
        cols, a, b = quarters[q], upper[q], lower[q]
        tsend[0, :, cols] = partial(3, q, pl.ds(0, ROWS)).astype(BF16)
        return ring_copy(0, q, 0, a, rs_in, pair), ring_copy(1, q, 0, b, rs_in, next_pair)

    def own_parts(q):
        cols, a, b = quarters[q], upper[q], lower[q]
        tnear[a, cols] = partial(2, q, a)
        tnear[b, cols] = partial(1, q, b)
        tfin[:, cols] = partial(0, q, pl.ds(0, ROWS))

    def send_sum(q, first):
        cols, a, b = quarters[q], upper[q], lower[q]
        with jax.named_scope(f"rs first wait {q}"):
            first[0].wait_recv()
        tsend[2, a, cols] = (tnear[a, cols] + rs_in[a, cols].astype(F32)).astype(BF16)
        one = ring_copy(0, q, 2, a, rs_n, next_pair)
        with jax.named_scope(f"rs first wait {q} b"):
            first[1].wait_recv()
        tsend[2, b, cols] = (tnear[b, cols] + rs_in[b, cols].astype(F32)).astype(BF16)
        return one, ring_copy(1, q, 2, b, rs_p, pair)

    def give_back(i, c):
        for m in range(4):
            part = pl.ds(m * 256, 256)
            send[2 + i, c, part, :] = nn(pack_m[part, :], ys[i, c]).astype(BF16)
        spread(2 + i, c)

    def stack_up(i, c, h, total):
        total = total.astype(BF16)
        for j in range(NSUB):
            ys[i, c, j * ROWS:(j + 1) * ROWS, h * 128:(h + 1) * 128] = total[:, j * 128:(j + 1) * 128]

    def give_back_quarter(q):
        c, lanes = q // 2, pl.ds(q % 2 * 128, 128)
        send[3, c, :, lanes] = nn(pack_m[...], ys[1, c, :, lanes]).astype(BF16)

        def one(d, carry):
            to = place(d)
            pltpu.make_async_remote_copy(
                src_ref=send.at[3, c, pl.ds(pl.multiple_of(to * BLK, BLK), BLK), lanes],
                dst_ref=recv.at[3, c, pl.ds(pl.multiple_of(e * BLK, BLK), BLK), lanes],
                send_sem=b_send.at[q], recv_sem=b_recv.at[q],
                device_id=(p, to * RING + k), device_id_type=MESH).start()
            return carry
        lax.fori_loop(1, NEXP, one, 0)
        own = pl.ds(pl.multiple_of(e * BLK, BLK), BLK)
        recv[3, c, own, lanes] = send[3, c, own, lanes]

    def whole_quarter(q):
        c, lanes = q // 2, pl.ds(q % 2 * 128, 128)
        part = pl.ds(0, PACK - BLK)
        return pltpu.make_async_remote_copy(
            src_ref=send.at[3, c, part, lanes], dst_ref=recv.at[3, c, part, lanes],
            send_sem=b_send.at[q], recv_sem=b_recv.at[q], device_id=pair, device_id_type=MESH)

    def pair_total(i, cols):
        return nn(hk[i], wd[0, :, cols]) + nn(hp[i], wd[1, :, cols])

    gate_f = as_column(gates_f[...].astype(BF16).astype(F32))
    gate_b = as_column(gates_b[...].astype(BF16).astype(F32))
    kept_wide = kept[...].astype(F32)
    inverse_b = lax.rsqrt(jnp.mean(kept_wide * kept_wide, axis=-1, keepdims=True) + EPS)

    def home_forward(c):
        with jax.named_scope(f"home f wait {c}"):
            if c == 0:
                pipe_f.wait_recv()
            whole(2, c).wait_recv()

        def one(j, carry):
            got = nn(get_m[0, pl.ds(pl.multiple_of(j * TOK, TOK), TOK), :], recv[2, c])
            for h in range(2):
                cols = col(c, h, j)
                out_f[:, cols] = (arr[:, cols].astype(F32) + gate_f * got[:, h * 128:(h + 1) * 128]).astype(BF16)
            return carry
        lax.fori_loop(0, NSUB, one, 0)

    def home_backward(q):
        with jax.named_scope(f"home b wait {q}"):
            whole_quarter(q).wait_recv()
        c, h = q // 2, q % 2

        got = nn(get_m[1], recv[3, c, :, h * 128:(h + 1) * 128])
        inner = jnp.zeros((TOK, 128), F32)
        for j in range(NSUB):
            cols = pl.ds((2 * c + h) * HALF + j * 128, 128)
            scaled = gate_b * got[j * TOK:(j + 1) * TOK] * gain_ref[:, cols]
            gnorm[:, cols] = scaled
            inner = inner + scaled * kept[:, cols].astype(F32)
        return inner

    def finish_sum(q):
        cols = quarters[q]
        with jax.named_scope(f"rs final wait {q}"):
            for copy in (singles_p[q], singles_n[q]) + summed[q]:
                copy.wait_recv()
        stack_up(1, q // 2, q % 2, tfin[:, cols] + rs_p[:, cols].astype(F32) + rs_n[:, cols].astype(F32))
        with jax.named_scope(f"give back b {q}"):
            give_back_quarter(q)

    with jax.named_scope("h pair wait"):
        h_p0.wait_recv()
        h_p1.wait_recv()
    h_n1 = remote(hp.at[1], hn.at[1], h_send.at[3], h_recv.at[3], next_pair)
    grad_group(0)
    with jax.named_scope("b rows wait"):
        b_rows.wait_recv()
        b_part.wait_recv()
    with jax.named_scope("gh 2"):
        ghb[2] = (nt(xbn[...], wd[0, :, F2]) + gpn[:, :HID].astype(F32)).astype(BF16)
        grad_group(2)
    with jax.named_scope("singles next"):
        singles_n = [send_single_next(q) for q in range(2)]
    with jax.named_scope("h next wait"):
        h_n0.wait_recv()
        h_n1.wait_recv()
    with jax.named_scope("out f 0"):
        for h in range(2):
            cols = half(0, h)
            stack_up(0, 0, h, pair_total(0, cols) + nn(hn[0], wd[2, :, cols]) + nn(hn[1], wd[3, :, cols]))
        give_back(0, 0)
    grad_pair = []
    for i, part in enumerate((HA, HB)):
        with jax.named_scope(f"wd F2 wait {i}"):
            w_f2[i].wait_recv()
        with jax.named_scope(f"gh pair {i}"):
            gsp[0, :, part] = nt(xb[...], wd[1, part, :]).astype(BF16)
            grad_pair.append(remote(gsp.at[0, :, part], ghb.at[1, :, part], g_send.at[2 + i], g_recv.at[2 + i], pair))
            other = pl.ds(HID + i * (HID // 2), HID // 2)
            gsp[1, :, part] = (nt(xbn[...], wd[1, part, F2]) + gpn[:, other].astype(F32)).astype(BF16)
            grad_pair.append(remote(gsp.at[1, :, part], ghb.at[3, :, part], g_send.at[4 + i], g_recv.at[4 + i], pair))
    with jax.named_scope("out f part"):
        for h in range(2):
            part = pl.ds(h * HALF, HALF)
            fs[:, part] = pair_total(1, half(1, h)).astype(BF16)
        f_part = remote(fs, fr, h_send.at[4], h_recv.at[4], next_pair)
    with jax.named_scope("gh pair wait"):
        for copy in grad_pair:
            copy.wait_recv()
    singles_p, firsts, summed = [], [], []
    with jax.named_scope("ring sums 0"):
        for r in (1, 3):
            grad_group(r)
        firsts.append(send_first(0))
        singles_p.append(send_single_pair(0))
    with jax.named_scope("ring sums 1"):
        for q in (1, 2):
            firsts.append(send_first(q))
            singles_p.append(send_single_pair(q))
        for q in range(2 * NCH):
            own_parts(q)
    with jax.named_scope("f part wait"):
        f_part.wait_recv()
    with jax.named_scope("out f 1"):
        for h in range(2):
            stack_up(0, 1, h, pair_total(0, half(1, h)) + fr[:, h * HALF:(h + 1) * HALF].astype(F32))
        give_back(0, 1)
    summed.append(send_sum(0, firsts[0]))
    summed.append(send_sum(1, firsts[1]))
    with jax.named_scope("ring sums 3"):
        singles_n.append(send_single_next(2))
        firsts.append(send_first(3))
    summed.append(send_sum(2, firsts[2]))
    with jax.named_scope("ring sums 4"):
        singles_p.append(send_single_pair(3))
        singles_n.append(send_single_next(3))
    finish_sum(0)
    summed.append(send_sum(3, firsts[3]))
    finish_sum(1)
    home_forward(0)
    finish_sum(2)
    home_forward(1)
    finish_sum(3)

    inner = home_backward(0)
    for q in range(1, 2 * NCH):
        inner = inner + home_backward(q)
    with jax.named_scope("final"):
        shift = inverse_b * inverse_b * jnp.sum(inner, axis=-1, keepdims=True) / D
        for q in range(2 * NCH):
            cols = quarters[q]
            out_b[:, cols] = (ret[:, cols].astype(F32) + inverse_b * (
                gnorm[:, cols] - kept[:, cols].astype(F32) * shift)).astype(BF16)

    for copy in pending:
        copy.wait_send()
    for i in range(3):
        for c in range(NCH):
            whole(i, c).wait_send()
    for q in range(2 * NCH):
        whole_quarter(q).wait_send()


def on_device(forward_inputs, forward_routes, forward_gates, backward_inputs, backward_cotangent, backward_routes,
              backward_gates, saved_preacts, norm_gain, gate_weight, up_weight, down_weight):
    vmem = pl.BlockSpec(memory_space=pltpu.VMEM)
    hbm = pl.BlockSpec(memory_space=pl.ANY)
    dma = pltpu.SemaphoreType.DMA
    out = jax.ShapeDtypeStruct((TOK, D), BF16)
    scratch = [
        pltpu.VMEM((TOK, D), BF16),
        pltpu.VMEM((TOK, D), BF16),
        pltpu.VMEM((TOK, D), BF16),
        pltpu.VMEM((RING * ROWS, 2 * HID), BF16),
        pltpu.VMEM((D, HID), BF16),
        pltpu.VMEM((D, HID), BF16),
        pltpu.VMEM((RING, HID, D), BF16),
        pltpu.VMEM((2, PACK, NSUB * TOK), BF16),
        pltpu.VMEM((2, NSUB * TOK, PACK), BF16),
        pltpu.VMEM((PACK, NSUB * ROWS), BF16),
        pltpu.VMEM((NSUB * ROWS, PACK), BF16),
        pltpu.VMEM((1, TOK), jnp.int32),
        pltpu.VMEM((1, D), F32),
        pltpu.VMEM((TOK, D), BF16),
        pltpu.VMEM((4, NCH, PACK, 256), BF16),
        pltpu.VMEM((4, NCH, PACK, 256), BF16),
        pltpu.VMEM((RING, ROWS, D), BF16),
        pltpu.VMEM((ROWS, D), BF16),
        pltpu.VMEM((ROWS, 2 * HALF), BF16),
        pltpu.VMEM((2, ROWS, HID), BF16),
        pltpu.VMEM((2, ROWS, HID), BF16),
        pltpu.VMEM((2, ROWS, HID), BF16),
        pltpu.VMEM((2, ROWS, HID), BF16),
        pltpu.VMEM((ROWS, 2 * HALF), BF16),
        pltpu.VMEM((ROWS, 2 * HALF), BF16),
        pltpu.VMEM((ROWS, 2 * HID), BF16),
        pltpu.VMEM((ROWS, 2 * HID), BF16),
        pltpu.VMEM((2, ROWS, HID), BF16),
        pltpu.VMEM((RING, ROWS, HID), BF16),
        pltpu.VMEM((RING, ROWS, 2 * HID), F32),
        pltpu.VMEM((RING, ROWS, 2 * HID), BF16),
        pltpu.VMEM((3, ROWS, D), BF16),
        pltpu.VMEM((ROWS, D), F32),
        pltpu.VMEM((ROWS, D), F32),
        pltpu.VMEM((ROWS, D), BF16),
        pltpu.VMEM((ROWS, D), BF16),
        pltpu.VMEM((ROWS, D), BF16),
        pltpu.VMEM((2, NCH, NSUB * ROWS, 256), BF16),
        pltpu.VMEM((TOK, D), F32),
        dma((6,)), dma((4,)), dma((4,)), dma((8,)), dma((8,)), dma((8,)), dma((8,)), dma((12,)), dma((12,)),
        dma((5,)), dma((5,)), dma((6,)), dma((6,)), dma((24,)), dma((24,)), dma((4,)), dma((4,)),
    ]
    call = pl.pallas_call(
        kernel,
        out_shape=(out, out),
        in_specs=[hbm, hbm, hbm, vmem, vmem, vmem, vmem, hbm, vmem, hbm, hbm, hbm],
        out_specs=(vmem, vmem),
        scratch_shapes=scratch,
        compiler_params=pltpu.CompilerParams(collective_id=0, has_side_effects=True,
                                             vmem_limit_bytes=62 * 2 ** 20),
        cost_estimate=pl.CostEstimate(flops=10 ** 10, bytes_accessed=2 * 10 ** 7, transcendentals=10 ** 6),
    )

    def row(values):
        return values.reshape(1, TOK)

    outputs, grads = call(
        forward_inputs[0], backward_cotangent[0], backward_inputs[0], row(forward_routes), row(forward_gates),
        row(backward_routes), row(backward_gates), saved_preacts[0, 0], norm_gain, gate_weight[0], up_weight[0],
        down_weight[0])
    return outputs[None], grads[None]


def solution(mesh):
    tokens = P("pipe", "ep", None)
    in_specs = (tokens,) * 7 + (P("pipe", "ep", None, None), P("pipe", None), P("pipe", None, "ep"),
                                P("pipe", None, "ep"), tokens)
    return jax.shard_map(on_device, mesh=mesh, in_specs=in_specs, out_specs=(tokens, tokens), check_vma=False)
```

```python
import functools
import jax
import jax.numpy as jnp
from jax import lax
from jax.experimental import pallas as pl
from jax.experimental.pallas import tpu as pltpu
from jax.sharding import PartitionSpec as P


RING = 4
NEXP = 16
TOK = 128
D = 3584
HID = 256
CAP = 9
ROWS = NEXP * CAP
NCH = 2
NSUB = 7
HALF = NSUB * 128
BLK = 64
PACK = NEXP * BLK
EPS = 1e-6
MESH = pl.DeviceIdType.MESH
F32 = jnp.float32
BF16 = jnp.bfloat16


def iota(shape, dim):
    return lax.broadcasted_iota(jnp.int32, shape, dim)


def nn(a, b):
    return lax.dot_general(a, b, (((1,), (0,)), ((), ())), preferred_element_type=F32)


def nt(a, b):
    return lax.dot_general(a, b, (((1,), (1,)), ((), ())), preferred_element_type=F32)


def hot(mask):
    return jnp.where(mask, 1.0, 0.0).astype(BF16)


def as_column(row):
    t0, t1 = iota((TOK, TOK), 0), iota((TOK, TOK), 1)
    return jnp.sum(jnp.where(t0 == t1, jnp.broadcast_to(row, (TOK, TOK)), 0.0), axis=1, keepdims=True)


def slot_places(routes):
    t0, t1 = iota((TOK, TOK), 0), iota((TOK, TOK), 1)
    row = routes.astype(F32)
    column = as_column(row)
    same = column == row
    col_before = jnp.sum(jnp.where(same & (t1 < t0), 1.0, 0.0), axis=1, keepdims=True)
    row_before = jnp.sum(jnp.where(same & (t0 < t1), 1.0, 0.0), axis=0, keepdims=True)
    col = column * BLK + col_before
    return (row * BLK + row_before).astype(jnp.int32), col.astype(jnp.int32)


def kernel(fin, cot, bin_hbm, routes_f, gates_f, routes_b, gates_b, saved_hbm, gain_ref, wg_hbm, wu_hbm, wd_hbm,
           out_f, out_b,
           arr, ret, kept, saved, wg, wu, wd, put, get_m, pack_m, unpack_m, next_routes, next_gain, normed, send, recv, xs, xb, xbn, hk, hs, hp,
           hn, fs, fr, gsn, gpn, gsp, ghb, factor, gj, tsend, tnear, tfin, rs_in, rs_p, rs_n, ys, gnorm,
           loc_sem, p_send, p_recv, w_send, w_recv, d_send, d_recv, a_send, a_recv, h_send, h_recv, g_send, g_recv,
           r_send, r_recv, b_send, b_recv):
    p, ep = lax.axis_index("pipe"), lax.axis_index("ep")
    e, k = ep // RING, ep % RING
    groups = (k, k + 1 - 2 * (k % 2), RING - 1 - k, (k + 2) % RING)
    pair, next_pair = (p, e * RING + groups[1]), (p, e * RING + groups[2])
    after, before = ((p + 1) % 4, ep), ((p + 3) % 4, ep)
    pending = []

    def remote(src, dst, ssem, rsem, device):
        copy = pltpu.make_async_remote_copy(src_ref=src, dst_ref=dst, send_sem=ssem, recv_sem=rsem, device_id=device,
                                            device_id_type=MESH)
        copy.start()
        pending.append(copy)
        return copy

    loads = [pltpu.make_async_copy(a, b, loc_sem.at[i]) for i, (a, b) in enumerate(
        ((fin, normed), (wd_hbm, wd.at[0]), (wg_hbm, wg), (wu_hbm, wu), (saved_hbm, saved), (bin_hbm, kept)))]
    for load in loads:
        load.start()

    barrier = pltpu.get_barrier_semaphore()

    def greet(d, carry):
        pl.semaphore_signal(barrier, inc=1, device_id=(p, (e + d) % NEXP * RING + k), device_id_type=MESH)
        return carry

    def greet_before(d, carry):
        pl.semaphore_signal(barrier, inc=1, device_id=((p + 3) % 4, (e + d) % NEXP * RING + k), device_id_type=MESH)
        return carry

    lax.fori_loop(1, NEXP, greet, 0)
    lax.fori_loop(0, NEXP, greet_before, 0)
    for device in (pair, next_pair, after):
        pl.semaphore_signal(barrier, inc=1, device_id=device, device_id_type=MESH)
    with jax.named_scope("barrier wait"):
        pl.semaphore_wait(barrier, NEXP - 1 + NEXP + 3)

    to_routes = remote(routes_f, next_routes, p_send.at[2], p_recv.at[2], before)
    to_gain = remote(gain_ref, next_gain, p_send.at[3], p_recv.at[3], before)
    pipe_b = remote(cot, ret, p_send.at[1], p_recv.at[1], before)
    HA, HB = pl.ds(0, HID // 2), pl.ds(HID // 2, HID // 2)
    F1, F2 = pl.ds(0, 2 * HALF), pl.ds(2 * HALF, 2 * HALF)
    w_pb = remote(wd_hbm.at[HB, F1], wd.at[1, HB, F1], w_send.at[0], w_recv.at[0], pair)
    w_na = remote(wd_hbm.at[HA, F1], wd.at[2, HA, F1], w_send.at[1], w_recv.at[1], next_pair)
    w_pa = remote(wd_hbm.at[HA, F1], wd.at[1, HA, F1], w_send.at[2], w_recv.at[2], pair)
    w_nb = remote(wd_hbm.at[HB, F1], wd.at[2, HB, F1], w_send.at[3], w_recv.at[3], next_pair)

    def put_matrix(i, places):
        def one(j, carry):
            put[i, :, pl.ds(pl.multiple_of(j * 128, 128), 128)] = hot(iota((PACK, TOK), 0) == places + j * CAP)
            return carry
        lax.fori_loop(0, NSUB, one, 0)

    def get_matrix(i, places):
        def one(j, carry):
            get_m[i, pl.ds(pl.multiple_of(j * 128, 128), 128), :] = hot(iota((TOK, PACK), 1) == places + j * CAP)
            return carry
        lax.fori_loop(0, NSUB, one, 0)

    def ninth(v):
        return (v * 57) >> 9

    def unpack_matrix():
        def one(j, carry):
            r = iota((ROWS, PACK), 0)
            unpack_m[pl.ds(pl.multiple_of(j * ROWS, 16), ROWS), :] = hot(
                iota((ROWS, PACK), 1) == ninth(r) * (BLK - CAP) + r + j * CAP)
            return carry
        lax.fori_loop(0, NSUB, one, 0)

    def pack_matrix():
        for j in range(NSUB):
            r = iota((PACK, ROWS), 1)
            pack_m[:, j * ROWS:(j + 1) * ROWS] = hot(
                iota((PACK, ROWS), 0) == ninth(r) * (BLK - CAP) + r + j * CAP)

    def place(d):
        odd = d % 2
        return (e + odd * ((d + 1) // 2) + (1 - odd) * (NEXP - d // 2)) % NEXP

    def spread(i, c):
        s = 2 * i + c
        section = (p + 1) % 4 if i == 0 else p

        own = pl.ds(pl.multiple_of(e * BLK, BLK), BLK)

        def block(to):
            pltpu.make_async_remote_copy(
                src_ref=send.at[i, c, pl.ds(pl.multiple_of(to * BLK, BLK), BLK)], dst_ref=recv.at[i, c, own],
                send_sem=d_send.at[s], recv_sem=d_recv.at[s],
                device_id=(section, to * RING + k), device_id_type=MESH).start()

        def one(d, carry):
            block(place(d))
            return carry
        lax.fori_loop(1, NEXP, one, 0)
        if i > 0:
            recv[i, c, own, :] = send[i, c, own, :]
        else:
            block(e)

    def whole(i, c):
        part = pl.ds(0, PACK if i == 0 else PACK - BLK)
        return pltpu.make_async_remote_copy(
            src_ref=send.at[i, c, part], dst_ref=recv.at[i, c, part],
            send_sem=d_send.at[2 * i + c], recv_sem=d_recv.at[2 * i + c], device_id=pair, device_id_type=MESH)

    def half(c, h):
        return pl.ds((2 * c + h) * HALF, HALF)

    def col(c, h, j):
        return pl.ds(pl.multiple_of((2 * c + h) * HALF + j * 128, 128), 128)

    def dispatch(i, values, order):
        for c in order:
            stack = jnp.concatenate([
                jnp.concatenate([values[:, (2 * c + h) * HALF + j * 128:(2 * c + h) * HALF + (j + 1) * 128]
                                 for h in range(2)], axis=1) for j in range(NSUB)], axis=0)
            for m in range(4):
                part = pl.ds(m * 256, 256)
                send[i, c, part, :] = nn(put[i, part, :], stack).astype(BF16)
            spread(i, c)

    def unpack(i, c, target):
        def one(j, carry):
            got = nn(unpack_m[pl.ds(pl.multiple_of(j * ROWS, 16), ROWS), :], recv[i, c]).astype(BF16)
            target[:, col(c, 0, j)] = got[:, :128]
            target[:, col(c, 1, j)] = got[:, 128:]
            return carry
        lax.fori_loop(0, NSUB, one, 0)

    def saved_factors(r):
        group = groups[r]
        q = iota((ROWS, NEXP * RING * CAP), 0)
        take = hot(iota((ROWS, NEXP * RING * CAP), 1) == ninth(q) * (RING - 1) * CAP + q + group * CAP)
        pre = nn(take, saved[...])
        gate, up = pre[:, :HID], pre[:, HID:]
        sigma = 1.0 / (1.0 + jnp.exp(-gate))
        factor[r, :, :HID] = up * sigma * (1.0 + gate * (1.0 - sigma))
        factor[r, :, HID:] = gate * sigma

    loads[0].wait()
    wide = normed[...].astype(F32)
    inverse = lax.rsqrt(jnp.mean(wide * wide, axis=-1, keepdims=True) + EPS)
    with jax.named_scope("routes wait"):
        to_routes.wait_recv()
        to_gain.wait_recv()
    put_matrix(0, slot_places(next_routes[...])[0])
    normed[...] = (wide * inverse * next_gain[...]).astype(BF16)
    with jax.named_scope("dispatch f"):
        dispatch(0, normed, (0, 1))

    cols_f = slot_places(routes_f[...])[1]
    rows_b, cols_b = slot_places(routes_b[...])
    put_matrix(1, rows_b)
    unpack_matrix()
    for load in loads[1:]:
        load.wait()
    with jax.named_scope("saved factors"):
        for r in range(RING):
            saved_factors(r)

    with jax.named_scope("wd fwd wait"):
        w_na.wait_recv()
    w_pf = remote(wd.at[2, HA, F1], wd.at[3, HA, F1], w_send.at[4], w_recv.at[4], pair)
    w_pb.wait_recv()
    w_nf = remote(wd.at[1, HB, F1], wd.at[3, HB, F1], w_send.at[5], w_recv.at[5], next_pair)

    def gather(c):
        with jax.named_scope(f"f disp wait {c}"):
            whole(0, c).wait_recv()
        unpack(0, c, xs.at[0])
        A, B = half(c, 0), half(c, 1)
        o = 6 * c
        x_pb = remote(xs.at[0, :, B], xs.at[1, :, B], a_send.at[o], a_recv.at[o], pair)
        x_na = remote(xs.at[0, :, A], xs.at[2, :, A], a_send.at[o + 1], a_recv.at[o + 1], next_pair)
        x_pa = remote(xs.at[0, :, A], xs.at[1, :, A], a_send.at[o + 2], a_recv.at[o + 2], pair)
        x_nb = remote(xs.at[0, :, B], xs.at[2, :, B], a_send.at[o + 3], a_recv.at[o + 3], next_pair)
        return x_pb, x_na, x_pa, x_nb

    def on_to_pair(c):
        A, o = half(c, 0), 6 * c + 4
        return remote(xs.at[2, :, A], xs.at[3, :, A], a_send.at[o], a_recv.at[o], pair)

    def on_to_next(c):
        B, o = half(c, 1), 6 * c + 5
        return remote(xs.at[1, :, B], xs.at[3, :, B], a_send.at[o], a_recv.at[o], next_pair)

    def hidden(r):
        rows = xs[r]
        pre_gate = nn(rows, wg[...])
        pre_up = nn(rows, wu[...])
        return (pre_gate / (1.0 + jnp.exp(-pre_gate)) * pre_up).astype(BF16)

    gathers = [gather(0)]

    with jax.named_scope("pipe b wait"):
        pipe_b.wait_recv()
    with jax.named_scope("dispatch b"):
        dispatch(1, ret, (1, 0))
    pipe_f = remote(fin, arr, p_send.at[0], p_recv.at[0], after)

    gathers.append(gather(1))
    with jax.named_scope("hidden 0"):
        hk[0] = hidden(0)

    with jax.named_scope("matrices"):
        pack_matrix()
        get_matrix(0, cols_f)
        get_matrix(1, cols_b)

    x_on = []
    for c in range(NCH):
        with jax.named_scope(f"x na pb wait {c}"):
            gathers[c][1].wait_recv()
            x_on.append(on_to_pair(c))
            gathers[c][0].wait_recv()
            x_on.append(on_to_next(c))

    def exchange_f2(i, rows):
        cols = (rows, F2)
        return remote(wd_hbm.at[cols], wd.at[(1,) + cols], w_send.at[6 + i], w_recv.at[6 + i], pair)

    with jax.named_scope("b disp wait 1"):
        whole(1, 1).wait_recv()
    unpack(1, 1, xb)
    b_rows = remote(xb.at[:, F2], xbn, g_send.at[0], g_recv.at[0], next_pair)
    w_f2 = [exchange_f2(0, HA)]
    with jax.named_scope("b disp wait 0"):
        whole(1, 0).wait_recv()
    unpack(1, 0, xb)
    with jax.named_scope("wd F1 wait"):
        for copy in (w_pa, w_nb, w_pf, w_nf):
            copy.wait_recv()
    with jax.named_scope("gh F1"):
        for r in (2, 3):
            gsn[:, (r - 2) * HID:(r - 1) * HID] = nt(xb[:, F1], wd[r, :, F1]).astype(BF16)
        b_part = remote(gsn, gpn, g_send.at[1], g_recv.at[1], next_pair)
        ghb[0] = nt(xb[...], wd[0]).astype(BF16)

    with jax.named_scope("x rest wait"):
        for c in range(NCH):
            gathers[c][2].wait_recv()
            gathers[c][3].wait_recv()
    with jax.named_scope("hidden 2 1"):
        hk[1] = hidden(2)
        h_n0 = remote(hk.at[1], hn.at[0], h_send.at[0], h_recv.at[0], next_pair)
        hs[0] = hidden(1)
        h_p0 = remote(hs.at[0], hp.at[0], h_send.at[1], h_recv.at[1], pair)
    with jax.named_scope("x on wait"):
        for copy in x_on:
            copy.wait_recv()
    with jax.named_scope("hidden 3"):
        hs[1] = hidden(3)
        h_p1 = remote(hs.at[1], hp.at[1], h_send.at[2], h_recv.at[2], pair)
    w_f2.append(exchange_f2(1, HB))

    def grad_group(r):
        grad = ghb[r].astype(F32)
        gj[r, :, :HID] = (grad * factor[r, :, :HID]).astype(BF16)
        gj[r, :, HID:] = (grad * factor[r, :, HID:]).astype(BF16)

    def partial(r, q, rows):
        cols = pl.ds(q * HALF, HALF)
        return nt(gj[r, rows, :HID], wg[cols, :]) + nt(gj[r, rows, HID:], wu[cols, :])

    quarters = [pl.ds(q * HALF, HALF) for q in range(2 * NCH)]
    cut = [80, 80, 80, 96]
    upper = [pl.ds(0, n) for n in cut]
    lower = [pl.ds(n, ROWS - n) for n in cut]

    def ring_copy(i, q, kind, rows, target, device):
        cols = quarters[q]
        n = 6 * q + 2 * kind + i
        return remote(tsend.at[kind, rows, cols], target.at[rows, cols], r_send.at[n], r_recv.at[n], device)

    def send_single_pair(q):
        cols, a = quarters[q], upper[q]
        tsend[1, a, cols] = partial(1, q, a).astype(BF16)
        return ring_copy(0, q, 1, a, rs_p, pair)

    def send_single_next(q):
        cols, b = quarters[q], lower[q]
        tsend[1, b, cols] = partial(2, q, b).astype(BF16)
        return ring_copy(1, q, 1, b, rs_n, next_pair)

    def send_first_pair(q):
        cols, a = quarters[q], upper[q]
        tsend[0, a, cols] = partial(3, q, a).astype(BF16)
        return ring_copy(0, q, 0, a, rs_in, pair)

    def send_first_next(q):
        cols, b = quarters[q], lower[q]
        tsend[0, b, cols] = partial(3, q, b).astype(BF16)
        return ring_copy(1, q, 0, b, rs_in, next_pair)

    def own_parts(q):
        cols, a, b = quarters[q], upper[q], lower[q]
        tnear[a, cols] = partial(2, q, a)
        tnear[b, cols] = partial(1, q, b)
        tfin[:, cols] = partial(0, q, pl.ds(0, ROWS))

    def send_sum(q):
        cols, a, b = quarters[q], upper[q], lower[q]
        with jax.named_scope(f"rs first wait {q}"):
            firsts_p[q].wait_recv()
        tsend[2, a, cols] = (tnear[a, cols] + rs_in[a, cols].astype(F32)).astype(BF16)
        one = ring_copy(0, q, 2, a, rs_n, next_pair)
        with jax.named_scope(f"rs first wait {q} b"):
            firsts_n[q].wait_recv()
        tsend[2, b, cols] = (tnear[b, cols] + rs_in[b, cols].astype(F32)).astype(BF16)
        return one, ring_copy(1, q, 2, b, rs_p, pair)

    def give_back(i, c):
        for m in range(4):
            part = pl.ds(m * 256, 256)
            send[2 + i, c, part, :] = nn(pack_m[part, :], ys[i, c]).astype(BF16)
        spread(2 + i, c)

    def stack_up(i, c, h, total):
        total = total.astype(BF16)
        for j in range(NSUB):
            ys[i, c, j * ROWS:(j + 1) * ROWS, h * 128:(h + 1) * 128] = total[:, j * 128:(j + 1) * 128]

    def give_back_quarter(q):
        c, lanes = q // 2, pl.ds(q % 2 * 128, 128)
        send[3, c, :, lanes] = nn(pack_m[...], ys[1, c, :, lanes]).astype(BF16)

        def one(d, carry):
            to = place(d)
            pltpu.make_async_remote_copy(
                src_ref=send.at[3, c, pl.ds(pl.multiple_of(to * BLK, BLK), BLK), lanes],
                dst_ref=recv.at[3, c, pl.ds(pl.multiple_of(e * BLK, BLK), BLK), lanes],
                send_sem=b_send.at[q], recv_sem=b_recv.at[q],
                device_id=(p, to * RING + k), device_id_type=MESH).start()
            return carry
        lax.fori_loop(1, NEXP, one, 0)
        own = pl.ds(pl.multiple_of(e * BLK, BLK), BLK)
        recv[3, c, own, lanes] = send[3, c, own, lanes]

    def whole_quarter(q):
        c, lanes = q // 2, pl.ds(q % 2 * 128, 128)
        part = pl.ds(0, PACK - BLK)
        return pltpu.make_async_remote_copy(
            src_ref=send.at[3, c, part, lanes], dst_ref=recv.at[3, c, part, lanes],
            send_sem=b_send.at[q], recv_sem=b_recv.at[q], device_id=pair, device_id_type=MESH)

    def pair_total(i, cols):
        return nn(hk[i], wd[0, :, cols]) + nn(hp[i], wd[1, :, cols])

    gate_f = as_column(gates_f[...].astype(BF16).astype(F32))
    gate_b = as_column(gates_b[...].astype(BF16).astype(F32))
    kept_wide = kept[...].astype(F32)
    inverse_b = lax.rsqrt(jnp.mean(kept_wide * kept_wide, axis=-1, keepdims=True) + EPS)

    def home_forward(c):
        with jax.named_scope(f"home f wait {c}"):
            if c == 0:
                pipe_f.wait_recv()
            whole(2, c).wait_recv()

        def one(j, carry):
            got = nn(get_m[0, pl.ds(pl.multiple_of(j * TOK, TOK), TOK), :], recv[2, c])
            for h in range(2):
                cols = col(c, h, j)
                out_f[:, cols] = (arr[:, cols].astype(F32) + gate_f * got[:, h * 128:(h + 1) * 128]).astype(BF16)
            return carry
        lax.fori_loop(0, NSUB, one, 0)

    def home_backward(q):
        with jax.named_scope(f"home b wait {q}"):
            whole_quarter(q).wait_recv()
        c, h = q // 2, q % 2

        got = nn(get_m[1], recv[3, c, :, h * 128:(h + 1) * 128])
        inner = jnp.zeros((TOK, 128), F32)
        for j in range(NSUB):
            cols = pl.ds((2 * c + h) * HALF + j * 128, 128)
            scaled = gate_b * got[j * TOK:(j + 1) * TOK] * gain_ref[:, cols]
            gnorm[:, cols] = scaled
            inner = inner + scaled * kept[:, cols].astype(F32)
        return inner

    def finish_sum(q):
        cols = quarters[q]
        with jax.named_scope(f"rs final wait {q}"):
            for copy in (singles_p[q], singles_n[q]) + summed[q]:
                copy.wait_recv()
        stack_up(1, q // 2, q % 2, tfin[:, cols] + rs_p[:, cols].astype(F32) + rs_n[:, cols].astype(F32))
        with jax.named_scope(f"give back b {q}"):
            give_back_quarter(q)

    with jax.named_scope("h pair wait"):
        h_p0.wait_recv()
        h_p1.wait_recv()
    h_n1 = remote(hp.at[1], hn.at[1], h_send.at[3], h_recv.at[3], next_pair)
    grad_group(0)
    with jax.named_scope("b rows wait"):
        b_rows.wait_recv()
        b_part.wait_recv()
    with jax.named_scope("gh 2"):
        ghb[2] = (nt(xbn[...], wd[0, :, F2]) + gpn[:, :HID].astype(F32)).astype(BF16)
        grad_group(2)
    with jax.named_scope("singles next"):
        singles_n = [send_single_next(q) for q in range(2)]
    with jax.named_scope("h next wait"):
        h_n0.wait_recv()
        h_n1.wait_recv()
    with jax.named_scope("out f 0"):
        for h in range(2):
            cols = half(0, h)
            stack_up(0, 0, h, pair_total(0, cols) + nn(hn[0], wd[2, :, cols]) + nn(hn[1], wd[3, :, cols]))
        give_back(0, 0)
    grad_pair = []
    for i, part in enumerate((HA, HB)):
        with jax.named_scope(f"wd F2 wait {i}"):
            w_f2[i].wait_recv()
        with jax.named_scope(f"gh pair {i}"):
            gsp[0, :, part] = nt(xb[...], wd[1, part, :]).astype(BF16)
            grad_pair.append(remote(gsp.at[0, :, part], ghb.at[1, :, part], g_send.at[2 + i], g_recv.at[2 + i], pair))
            other = pl.ds(HID + i * (HID // 2), HID // 2)
            gsp[1, :, part] = (nt(xbn[...], wd[1, part, F2]) + gpn[:, other].astype(F32)).astype(BF16)
            grad_pair.append(remote(gsp.at[1, :, part], ghb.at[3, :, part], g_send.at[4 + i], g_recv.at[4 + i], pair))
    with jax.named_scope("out f part"):
        for h in range(2):
            part = pl.ds(h * HALF, HALF)
            fs[:, part] = pair_total(1, half(1, h)).astype(BF16)
        f_part = remote(fs, fr, h_send.at[4], h_recv.at[4], next_pair)
    with jax.named_scope("gh pair wait"):
        for copy in grad_pair:
            copy.wait_recv()
    singles_p, firsts_p, firsts_n, summed = [], [], [], []
    with jax.named_scope("ring sums 0"):
        for r in (1, 3):
            grad_group(r)
        firsts_n.append(send_first_next(0))
        firsts_p.append(send_first_pair(0))
        singles_p.append(send_single_pair(0))
    with jax.named_scope("ring sums 1"):
        firsts_n.append(send_first_next(1))
        firsts_p.append(send_first_pair(1))
        singles_p.append(send_single_pair(1))
        firsts_p.append(send_first_pair(2))
        for q in range(2 * NCH):
            own_parts(q)
    with jax.named_scope("f part wait"):
        f_part.wait_recv()
    with jax.named_scope("out f 1"):
        for h in range(2):
            stack_up(0, 1, h, pair_total(0, half(1, h)) + fr[:, h * HALF:(h + 1) * HALF].astype(F32))
        give_back(0, 1)
    for q in range(2):
        summed.append(send_sum(q))
    with jax.named_scope("first 2 3"):
        firsts_n.append(send_first_next(2))
        singles_p.append(send_single_pair(2))
        singles_n.append(send_single_next(2))
        firsts_p.append(send_first_pair(3))
        firsts_n.append(send_first_next(3))
    for q in range(2):
        finish_sum(q)
    summed.append(send_sum(2))
    singles_p.append(send_single_pair(3))
    singles_n.append(send_single_next(3))
    summed.append(send_sum(3))
    home_forward(0)
    finish_sum(2)
    home_forward(1)
    finish_sum(3)

    inner = home_backward(0)
    for q in range(1, 2 * NCH):
        inner = inner + home_backward(q)
    with jax.named_scope("final"):
        shift = inverse_b * inverse_b * jnp.sum(inner, axis=-1, keepdims=True) / D
        for q in range(2 * NCH):
            cols = quarters[q]
            out_b[:, cols] = (ret[:, cols].astype(F32) + inverse_b * (
                gnorm[:, cols] - kept[:, cols].astype(F32) * shift)).astype(BF16)

    for copy in pending:
        copy.wait_send()
    for i in range(3):
        for c in range(NCH):
            whole(i, c).wait_send()
    for q in range(2 * NCH):
        whole_quarter(q).wait_send()


def on_device(forward_inputs, forward_routes, forward_gates, backward_inputs, backward_cotangent, backward_routes,
              backward_gates, saved_preacts, norm_gain, gate_weight, up_weight, down_weight):
    vmem = pl.BlockSpec(memory_space=pltpu.VMEM)
    hbm = pl.BlockSpec(memory_space=pl.ANY)
    dma = pltpu.SemaphoreType.DMA
    out = pltpu.VMEM((TOK, D), BF16)
    scratch = [
        pltpu.VMEM((TOK, D), BF16),
        pltpu.VMEM((TOK, D), BF16),
        pltpu.VMEM((TOK, D), BF16),
        pltpu.VMEM((RING * ROWS, 2 * HID), BF16),
        pltpu.VMEM((D, HID), BF16),
        pltpu.VMEM((D, HID), BF16),
        pltpu.VMEM((RING, HID, D), BF16),
        pltpu.VMEM((2, PACK, NSUB * TOK), BF16),
        pltpu.VMEM((2, NSUB * TOK, PACK), BF16),
        pltpu.VMEM((PACK, NSUB * ROWS), BF16),
        pltpu.VMEM((NSUB * ROWS, PACK), BF16),
        pltpu.VMEM((1, TOK), jnp.int32),
        pltpu.VMEM((1, D), F32),
        pltpu.VMEM((TOK, D), BF16),
        pltpu.VMEM((4, NCH, PACK, 256), BF16),
        pltpu.VMEM((4, NCH, PACK, 256), BF16),
        pltpu.VMEM((RING, ROWS, D), BF16),
        pltpu.VMEM((ROWS, D), BF16),
        pltpu.VMEM((ROWS, 2 * HALF), BF16),
        pltpu.VMEM((2, ROWS, HID), BF16),
        pltpu.VMEM((2, ROWS, HID), BF16),
        pltpu.VMEM((2, ROWS, HID), BF16),
        pltpu.VMEM((2, ROWS, HID), BF16),
        pltpu.VMEM((ROWS, 2 * HALF), BF16),
        pltpu.VMEM((ROWS, 2 * HALF), BF16),
        pltpu.VMEM((ROWS, 2 * HID), BF16),
        pltpu.VMEM((ROWS, 2 * HID), BF16),
        pltpu.VMEM((2, ROWS, HID), BF16),
        pltpu.VMEM((RING, ROWS, HID), BF16),
        pltpu.VMEM((RING, ROWS, 2 * HID), F32),
        pltpu.VMEM((RING, ROWS, 2 * HID), BF16),
        pltpu.VMEM((3, ROWS, D), BF16),
        pltpu.VMEM((ROWS, D), F32),
        pltpu.VMEM((ROWS, D), F32),
        pltpu.VMEM((ROWS, D), BF16),
        pltpu.VMEM((ROWS, D), BF16),
        pltpu.VMEM((ROWS, D), BF16),
        pltpu.VMEM((2, NCH, NSUB * ROWS, 256), BF16),
        pltpu.VMEM((TOK, D), F32),
        dma((6,)), dma((4,)), dma((4,)), dma((8,)), dma((8,)), dma((8,)), dma((8,)), dma((12,)), dma((12,)),
        dma((5,)), dma((5,)), dma((6,)), dma((6,)), dma((24,)), dma((24,)), dma((4,)), dma((4,)),
    ]
    call = pl.pallas_call(
        kernel,
        out_shape=(out, out),
        in_specs=[hbm, hbm, hbm, vmem, vmem, vmem, vmem, hbm, vmem, hbm, hbm, hbm],
        out_specs=(vmem, vmem),
        scratch_shapes=scratch,
        compiler_params=pltpu.CompilerParams(collective_id=0, has_side_effects=True,
                                             vmem_limit_bytes=62 * 2 ** 20),
        cost_estimate=pl.CostEstimate(flops=10 ** 10, bytes_accessed=2 * 10 ** 7, transcendentals=10 ** 6),
    )

    def row(values):
        return values.reshape(1, TOK)

    outputs, grads = call(
        forward_inputs[0], backward_cotangent[0], backward_inputs[0], row(forward_routes), row(forward_gates),
        row(backward_routes), row(backward_gates), saved_preacts[0, 0], norm_gain, gate_weight[0], up_weight[0],
        down_weight[0])
    return outputs[None], grads[None]


def solution(mesh):
    tokens = P("pipe", "ep", None)
    in_specs = (tokens,) * 7 + (P("pipe", "ep", None, None), P("pipe", None), P("pipe", None, "ep"),
                                P("pipe", None, "ep"), tokens)
    return jax.shard_map(on_device, mesh=mesh, in_specs=in_specs, out_specs=(tokens, tokens), check_vma=False)
```

```python
import functools
import jax
import jax.numpy as jnp
from jax import lax
from jax.experimental import pallas as pl
from jax.experimental.pallas import tpu as pltpu
from jax.sharding import PartitionSpec as P


RING = 4
NEXP = 16
TOK = 128
D = 3584
HID = 256
CAP = 9
ROWS = NEXP * CAP
NCH = 2
NSUB = 7
HALF = NSUB * 128
BLK = 64
PACK = NEXP * BLK
EPS = 1e-6
MESH = pl.DeviceIdType.MESH
F32 = jnp.float32
BF16 = jnp.bfloat16


def iota(shape, dim):
    return lax.broadcasted_iota(jnp.int32, shape, dim)


def nn(a, b):
    return lax.dot_general(a, b, (((1,), (0,)), ((), ())), preferred_element_type=F32)


def nt(a, b):
    return lax.dot_general(a, b, (((1,), (1,)), ((), ())), preferred_element_type=F32)


def hot(mask):
    return jnp.where(mask, 1.0, 0.0).astype(BF16)


def as_column(row):
    t0, t1 = iota((TOK, TOK), 0), iota((TOK, TOK), 1)
    return jnp.sum(jnp.where(t0 == t1, jnp.broadcast_to(row, (TOK, TOK)), 0.0), axis=1, keepdims=True)


def slot_places(routes):
    t0, t1 = iota((TOK, TOK), 0), iota((TOK, TOK), 1)
    row = routes.astype(F32)
    column = as_column(row)
    same = column == row
    col_before = jnp.sum(jnp.where(same & (t1 < t0), 1.0, 0.0), axis=1, keepdims=True)
    row_before = jnp.sum(jnp.where(same & (t0 < t1), 1.0, 0.0), axis=0, keepdims=True)
    col = column * BLK + col_before
    return (row * BLK + row_before).astype(jnp.int32), col.astype(jnp.int32)


def kernel(fin, cot, bin_hbm, routes_f, gates_f, routes_b, gates_b, saved_hbm, gain_ref, wg_hbm, wu_hbm, wd_hbm,
           out_f, out_b,
           arr, ret, kept, saved, wg, wu, wd, put, get_m, pack_m, unpack_m, next_routes, next_gain, normed, send, recv, xs, xb, xbn, hk, hs, hp,
           hn, fs, fr, gsn, gpn, gsp, ghb, factor, gj, tsend, tnear, tfin, rs_in, rs_p, rs_n, ys, gnorm,
           loc_sem, p_send, p_recv, w_send, w_recv, d_send, d_recv, a_send, a_recv, h_send, h_recv, g_send, g_recv,
           r_send, r_recv, b_send, b_recv):
    p, ep = lax.axis_index("pipe"), lax.axis_index("ep")
    e, k = ep // RING, ep % RING
    groups = (k, k + 1 - 2 * (k % 2), RING - 1 - k, (k + 2) % RING)
    pair, next_pair = (p, e * RING + groups[1]), (p, e * RING + groups[2])
    after, before = ((p + 1) % 4, ep), ((p + 3) % 4, ep)
    pending = []

    def remote(src, dst, ssem, rsem, device):
        copy = pltpu.make_async_remote_copy(src_ref=src, dst_ref=dst, send_sem=ssem, recv_sem=rsem, device_id=device,
                                            device_id_type=MESH)
        copy.start()
        pending.append(copy)
        return copy

    loads = [pltpu.make_async_copy(a, b, loc_sem.at[i]) for i, (a, b) in enumerate(
        ((fin, normed), (wd_hbm, wd.at[0]), (wg_hbm, wg), (wu_hbm, wu), (saved_hbm, saved), (bin_hbm, kept)))]
    for load in loads:
        load.start()

    barrier = pltpu.get_barrier_semaphore()

    def greet(d, carry):
        pl.semaphore_signal(barrier, inc=1, device_id=(p, (e + d) % NEXP * RING + k), device_id_type=MESH)
        return carry

    def greet_before(d, carry):
        pl.semaphore_signal(barrier, inc=1, device_id=((p + 3) % 4, (e + d) % NEXP * RING + k), device_id_type=MESH)
        return carry

    lax.fori_loop(1, NEXP, greet, 0)
    lax.fori_loop(0, NEXP, greet_before, 0)
    for device in (pair, next_pair, after):
        pl.semaphore_signal(barrier, inc=1, device_id=device, device_id_type=MESH)
    with jax.named_scope("barrier wait"):
        pl.semaphore_wait(barrier, NEXP - 1 + NEXP + 3)

    to_routes = remote(routes_f, next_routes, p_send.at[2], p_recv.at[2], before)
    to_gain = remote(gain_ref, next_gain, p_send.at[3], p_recv.at[3], before)
    pipe_b = remote(cot, ret, p_send.at[1], p_recv.at[1], before)
    HA, HB = pl.ds(0, HID // 2), pl.ds(HID // 2, HID // 2)
    F1, F2 = pl.ds(0, 2 * HALF), pl.ds(2 * HALF, 2 * HALF)
    w_pb = remote(wd_hbm.at[HB, F1], wd.at[1, HB, F1], w_send.at[0], w_recv.at[0], pair)
    w_na = remote(wd_hbm.at[HA, F1], wd.at[2, HA, F1], w_send.at[1], w_recv.at[1], next_pair)
    w_pa = remote(wd_hbm.at[HA, F1], wd.at[1, HA, F1], w_send.at[2], w_recv.at[2], pair)
    w_nb = remote(wd_hbm.at[HB, F1], wd.at[2, HB, F1], w_send.at[3], w_recv.at[3], next_pair)

    def put_matrix(i, places):
        def one(j, carry):
            put[i, :, pl.ds(pl.multiple_of(j * 128, 128), 128)] = hot(iota((PACK, TOK), 0) == places + j * CAP)
            return carry
        lax.fori_loop(0, NSUB, one, 0)

    def get_matrix(i, places):
        def one(j, carry):
            get_m[i, pl.ds(pl.multiple_of(j * 128, 128), 128), :] = hot(iota((TOK, PACK), 1) == places + j * CAP)
            return carry
        lax.fori_loop(0, NSUB, one, 0)

    def ninth(v):
        return (v * 57) >> 9

    def unpack_matrix():
        def one(j, carry):
            r = iota((ROWS, PACK), 0)
            unpack_m[pl.ds(pl.multiple_of(j * ROWS, 16), ROWS), :] = hot(
                iota((ROWS, PACK), 1) == ninth(r) * (BLK - CAP) + r + j * CAP)
            return carry
        lax.fori_loop(0, NSUB, one, 0)

    def pack_matrix():
        for j in range(NSUB):
            r = iota((PACK, ROWS), 1)
            pack_m[:, j * ROWS:(j + 1) * ROWS] = hot(
                iota((PACK, ROWS), 0) == ninth(r) * (BLK - CAP) + r + j * CAP)

    def place(d):
        odd = d % 2
        return (e + odd * ((d + 1) // 2) + (1 - odd) * (NEXP - d // 2)) % NEXP

    def spread(i, c):
        s = 2 * i + c
        section = (p + 1) % 4 if i == 0 else p

        own = pl.ds(pl.multiple_of(e * BLK, BLK), BLK)

        def block(to):
            pltpu.make_async_remote_copy(
                src_ref=send.at[i, c, pl.ds(pl.multiple_of(to * BLK, BLK), BLK)], dst_ref=recv.at[i, c, own],
                send_sem=d_send.at[s], recv_sem=d_recv.at[s],
                device_id=(section, to * RING + k), device_id_type=MESH).start()

        def one(d, carry):
            block(place(d))
            return carry
        lax.fori_loop(1, NEXP, one, 0)
        if i > 0:
            recv[i, c, own, :] = send[i, c, own, :]
        else:
            block(e)

    def whole(i, c):
        part = pl.ds(0, PACK if i == 0 else PACK - BLK)
        return pltpu.make_async_remote_copy(
            src_ref=send.at[i, c, part], dst_ref=recv.at[i, c, part],
            send_sem=d_send.at[2 * i + c], recv_sem=d_recv.at[2 * i + c], device_id=pair, device_id_type=MESH)

    def half(c, h):
        return pl.ds((2 * c + h) * HALF, HALF)

    def col(c, h, j):
        return pl.ds(pl.multiple_of((2 * c + h) * HALF + j * 128, 128), 128)

    def dispatch(i, values, order):
        for c in order:
            stack = jnp.concatenate([
                jnp.concatenate([values[:, (2 * c + h) * HALF + j * 128:(2 * c + h) * HALF + (j + 1) * 128]
                                 for h in range(2)], axis=1) for j in range(NSUB)], axis=0)
            for m in range(4):
                part = pl.ds(m * 256, 256)
                send[i, c, part, :] = nn(put[i, part, :], stack).astype(BF16)
            spread(i, c)

    def unpack(i, c, target):
        def one(j, carry):
            got = nn(unpack_m[pl.ds(pl.multiple_of(j * ROWS, 16), ROWS), :], recv[i, c]).astype(BF16)
            target[:, col(c, 0, j)] = got[:, :128]
            target[:, col(c, 1, j)] = got[:, 128:]
            return carry
        lax.fori_loop(0, NSUB, one, 0)

    def saved_factors(r):
        group = groups[r]
        q = iota((ROWS, NEXP * RING * CAP), 0)
        take = hot(iota((ROWS, NEXP * RING * CAP), 1) == ninth(q) * (RING - 1) * CAP + q + group * CAP)
        pre = nn(take, saved[...])
        gate, up = pre[:, :HID], pre[:, HID:]
        sigma = 1.0 / (1.0 + jnp.exp(-gate))
        factor[r, :, :HID] = up * sigma * (1.0 + gate * (1.0 - sigma))
        factor[r, :, HID:] = gate * sigma

    loads[0].wait()
    wide = normed[...].astype(F32)
    inverse = lax.rsqrt(jnp.mean(wide * wide, axis=-1, keepdims=True) + EPS)
    with jax.named_scope("routes wait"):
        to_routes.wait_recv()
        to_gain.wait_recv()
    put_matrix(0, slot_places(next_routes[...])[0])
    normed[...] = (wide * inverse * next_gain[...]).astype(BF16)
    with jax.named_scope("dispatch f"):
        dispatch(0, normed, (0, 1))

    cols_f = slot_places(routes_f[...])[1]
    rows_b, cols_b = slot_places(routes_b[...])
    put_matrix(1, rows_b)
    unpack_matrix()
    for load in loads[1:]:
        load.wait()
    with jax.named_scope("saved factors"):
        for r in range(RING):
            saved_factors(r)

    with jax.named_scope("wd fwd wait"):
        w_na.wait_recv()
    w_pf = remote(wd.at[2, HA, F1], wd.at[3, HA, F1], w_send.at[4], w_recv.at[4], pair)
    w_pb.wait_recv()
    w_nf = remote(wd.at[1, HB, F1], wd.at[3, HB, F1], w_send.at[5], w_recv.at[5], next_pair)

    def gather(c):
        with jax.named_scope(f"f disp wait {c}"):
            whole(0, c).wait_recv()
        unpack(0, c, xs.at[0])
        A, B = half(c, 0), half(c, 1)
        o = 6 * c
        x_pb = remote(xs.at[0, :, B], xs.at[1, :, B], a_send.at[o], a_recv.at[o], pair)
        x_na = remote(xs.at[0, :, A], xs.at[2, :, A], a_send.at[o + 1], a_recv.at[o + 1], next_pair)
        x_pa = remote(xs.at[0, :, A], xs.at[1, :, A], a_send.at[o + 2], a_recv.at[o + 2], pair)
        x_nb = remote(xs.at[0, :, B], xs.at[2, :, B], a_send.at[o + 3], a_recv.at[o + 3], next_pair)
        return x_pb, x_na, x_pa, x_nb

    def on_to_pair(c):
        A, o = half(c, 0), 6 * c + 4
        return remote(xs.at[2, :, A], xs.at[3, :, A], a_send.at[o], a_recv.at[o], pair)

    def on_to_next(c):
        B, o = half(c, 1), 6 * c + 5
        return remote(xs.at[1, :, B], xs.at[3, :, B], a_send.at[o], a_recv.at[o], next_pair)

    def hidden(r):
        rows = xs[r]
        pre_gate = nn(rows, wg[...])
        pre_up = nn(rows, wu[...])
        return (pre_gate / (1.0 + jnp.exp(-pre_gate)) * pre_up).astype(BF16)

    gathers = [gather(0)]

    with jax.named_scope("pipe b wait"):
        pipe_b.wait_recv()
    with jax.named_scope("dispatch b"):
        dispatch(1, ret, (1, 0))
    pipe_f = remote(fin, arr, p_send.at[0], p_recv.at[0], after)

    gathers.append(gather(1))
    with jax.named_scope("hidden 0"):
        hk[0] = hidden(0)

    with jax.named_scope("matrices"):
        pack_matrix()
        get_matrix(0, cols_f)
        get_matrix(1, cols_b)

    x_on = []
    for c in range(NCH):
        with jax.named_scope(f"x na pb wait {c}"):
            gathers[c][1].wait_recv()
            x_on.append(on_to_pair(c))
            gathers[c][0].wait_recv()
            x_on.append(on_to_next(c))

    def exchange_f2(i, rows):
        cols = (rows, F2)
        return remote(wd_hbm.at[cols], wd.at[(1,) + cols], w_send.at[6 + i], w_recv.at[6 + i], pair)

    with jax.named_scope("b disp wait 1"):
        whole(1, 1).wait_recv()
    unpack(1, 1, xb)
    b_rows = remote(xb.at[:, F2], xbn, g_send.at[0], g_recv.at[0], next_pair)
    w_f2 = [exchange_f2(0, HA)]
    with jax.named_scope("b disp wait 0"):
        whole(1, 0).wait_recv()
    unpack(1, 0, xb)
    with jax.named_scope("wd F1 wait"):
        for copy in (w_pa, w_nb, w_pf, w_nf):
            copy.wait_recv()
    with jax.named_scope("gh F1"):
        for r in (2, 3):
            gsn[:, (r - 2) * HID:(r - 1) * HID] = nt(xb[:, F1], wd[r, :, F1]).astype(BF16)
        b_part = remote(gsn, gpn, g_send.at[1], g_recv.at[1], next_pair)
        ghb[0] = nt(xb[...], wd[0]).astype(BF16)

    with jax.named_scope("x rest wait"):
        for c in range(NCH):
            gathers[c][2].wait_recv()
            gathers[c][3].wait_recv()
    with jax.named_scope("hidden 2 1"):
        hk[1] = hidden(2)
        h_n0 = remote(hk.at[1], hn.at[0], h_send.at[0], h_recv.at[0], next_pair)
        hs[0] = hidden(1)
        h_p0 = remote(hs.at[0], hp.at[0], h_send.at[1], h_recv.at[1], pair)
    with jax.named_scope("x on wait"):
        for copy in x_on:
            copy.wait_recv()
    with jax.named_scope("hidden 3"):
        hs[1] = hidden(3)
        h_p1 = remote(hs.at[1], hp.at[1], h_send.at[2], h_recv.at[2], pair)
    w_f2.append(exchange_f2(1, HB))

    def grad_group(r):
        grad = ghb[r].astype(F32)
        gj[r, :, :HID] = (grad * factor[r, :, :HID]).astype(BF16)
        gj[r, :, HID:] = (grad * factor[r, :, HID:]).astype(BF16)

    def partial(r, q, rows):
        cols = pl.ds(q * HALF, HALF)
        return nt(gj[r, rows, :HID], wg[cols, :]) + nt(gj[r, rows, HID:], wu[cols, :])

    quarters = [pl.ds(q * HALF, HALF) for q in range(2 * NCH)]
    cut = [80, 80, 80, 80]
    upper = [pl.ds(0, n) for n in cut]
    lower = [pl.ds(n, ROWS - n) for n in cut]

    def ring_copy(i, q, kind, rows, target, device):
        cols = quarters[q]
        n = 6 * q + 2 * kind + i
        return remote(tsend.at[kind, rows, cols], target.at[rows, cols], r_send.at[n], r_recv.at[n], device)

    def send_single_pair(q):
        cols, a = quarters[q], upper[q]
        tsend[1, a, cols] = partial(1, q, a).astype(BF16)
        return ring_copy(0, q, 1, a, rs_p, pair)

    def send_single_next(q):
        cols, b = quarters[q], lower[q]
        tsend[1, b, cols] = partial(2, q, b).astype(BF16)
        return ring_copy(1, q, 1, b, rs_n, next_pair)

    def send_first_pair(q):
        cols, a = quarters[q], upper[q]
        tsend[0, a, cols] = partial(3, q, a).astype(BF16)
        return ring_copy(0, q, 0, a, rs_in, pair)

    def send_first_next(q):
        cols, b = quarters[q], lower[q]
        tsend[0, b, cols] = partial(3, q, b).astype(BF16)
        return ring_copy(1, q, 0, b, rs_in, next_pair)

    def own_parts(q):
        cols, a, b = quarters[q], upper[q], lower[q]
        tnear[a, cols] = partial(2, q, a)
        tnear[b, cols] = partial(1, q, b)
        tfin[:, cols] = partial(0, q, pl.ds(0, ROWS))

    def send_sum(q):
        cols, a, b = quarters[q], upper[q], lower[q]
        with jax.named_scope(f"rs first wait {q}"):
            firsts_p[q].wait_recv()
        tsend[2, a, cols] = (tnear[a, cols] + rs_in[a, cols].astype(F32)).astype(BF16)
        one = ring_copy(0, q, 2, a, rs_n, next_pair)
        with jax.named_scope(f"rs first wait {q} b"):
            firsts_n[q].wait_recv()
        tsend[2, b, cols] = (tnear[b, cols] + rs_in[b, cols].astype(F32)).astype(BF16)
        return one, ring_copy(1, q, 2, b, rs_p, pair)

    def give_back(i, c):
        for m in range(4):
            part = pl.ds(m * 256, 256)
            send[2 + i, c, part, :] = nn(pack_m[part, :], ys[i, c]).astype(BF16)
        spread(2 + i, c)

    def stack_up(i, c, h, total):
        total = total.astype(BF16)
        for j in range(NSUB):
            ys[i, c, j * ROWS:(j + 1) * ROWS, h * 128:(h + 1) * 128] = total[:, j * 128:(j + 1) * 128]

    def quarter_of(n):
        return (3, 1, n // 2, pl.ds(n % 2 * 128, 128)) if n < 4 else (2, 0, 1, pl.ds(n % 2 * 128, 128))

    def give_back_quarter(n):
        i, y, c, lanes = quarter_of(n)
        send[i, c, :, lanes] = nn(pack_m[...], ys[y, c, :, lanes]).astype(BF16)
        own = pl.ds(pl.multiple_of(e * BLK, BLK), BLK)

        def one(d, carry):
            to = place(d)
            pltpu.make_async_remote_copy(
                src_ref=send.at[i, c, pl.ds(pl.multiple_of(to * BLK, BLK), BLK), lanes],
                dst_ref=recv.at[i, c, own, lanes],
                send_sem=b_send.at[n], recv_sem=b_recv.at[n],
                device_id=(p, to * RING + k), device_id_type=MESH).start()
            return carry
        lax.fori_loop(1, NEXP, one, 0)
        recv[i, c, own, lanes] = send[i, c, own, lanes]

    def whole_quarter(n):
        i, y, c, lanes = quarter_of(n)
        part = pl.ds(0, PACK - BLK)
        return pltpu.make_async_remote_copy(
            src_ref=send.at[i, c, part, lanes], dst_ref=recv.at[i, c, part, lanes],
            send_sem=b_send.at[n], recv_sem=b_recv.at[n], device_id=pair, device_id_type=MESH)

    def pair_total(i, cols):
        return nn(hk[i], wd[0, :, cols]) + nn(hp[i], wd[1, :, cols])

    gate_f = as_column(gates_f[...].astype(BF16).astype(F32))
    gate_b = as_column(gates_b[...].astype(BF16).astype(F32))
    kept_wide = kept[...].astype(F32)
    inverse_b = lax.rsqrt(jnp.mean(kept_wide * kept_wide, axis=-1, keepdims=True) + EPS)

    def home_forward(c):
        with jax.named_scope(f"home f wait {c}"):
            if c == 0:
                pipe_f.wait_recv()
                whole(2, 0).wait_recv()
            else:
                whole_quarter(4).wait_recv()
                whole_quarter(5).wait_recv()

        def one(j, carry):
            got = nn(get_m[0, pl.ds(pl.multiple_of(j * TOK, TOK), TOK), :], recv[2, c])
            for h in range(2):
                cols = col(c, h, j)
                out_f[:, cols] = (arr[:, cols].astype(F32) + gate_f * got[:, h * 128:(h + 1) * 128]).astype(BF16)
            return carry
        lax.fori_loop(0, NSUB, one, 0)

    def home_backward(q):
        with jax.named_scope(f"home b wait {q}"):
            whole_quarter(q).wait_recv()
        c, h = q // 2, q % 2

        got = nn(get_m[1], recv[3, c, :, h * 128:(h + 1) * 128])
        inner = jnp.zeros((TOK, 128), F32)
        for j in range(NSUB):
            cols = pl.ds((2 * c + h) * HALF + j * 128, 128)
            scaled = gate_b * got[j * TOK:(j + 1) * TOK] * gain_ref[:, cols]
            gnorm[:, cols] = scaled
            inner = inner + scaled * kept[:, cols].astype(F32)
        return inner

    def finish_sum(q):
        cols = quarters[q]
        with jax.named_scope(f"rs final wait {q}"):
            for copy in (singles_p[q], singles_n[q]) + summed[q]:
                copy.wait_recv()
        stack_up(1, q // 2, q % 2, tfin[:, cols] + rs_p[:, cols].astype(F32) + rs_n[:, cols].astype(F32))
        with jax.named_scope(f"give back b {q}"):
            give_back_quarter(q)

    with jax.named_scope("h pair wait"):
        h_p0.wait_recv()
        h_p1.wait_recv()
    h_n1 = remote(hp.at[1], hn.at[1], h_send.at[3], h_recv.at[3], next_pair)
    grad_group(0)
    with jax.named_scope("b rows wait"):
        b_rows.wait_recv()
        b_part.wait_recv()
    with jax.named_scope("gh 2"):
        ghb[2] = (nt(xbn[...], wd[0, :, F2]) + gpn[:, :HID].astype(F32)).astype(BF16)
        grad_group(2)
    with jax.named_scope("singles next"):
        singles_n = [send_single_next(q) for q in range(2)]
    with jax.named_scope("h next wait"):
        h_n0.wait_recv()
        h_n1.wait_recv()
    with jax.named_scope("out f 0"):
        for h in range(2):
            cols = half(0, h)
            stack_up(0, 0, h, pair_total(0, cols) + nn(hn[0], wd[2, :, cols]) + nn(hn[1], wd[3, :, cols]))
        give_back(0, 0)
    grad_pair = []
    for i, part in enumerate((HA, HB)):
        with jax.named_scope(f"wd F2 wait {i}"):
            w_f2[i].wait_recv()
        with jax.named_scope(f"gh pair {i}"):
            gsp[0, :, part] = nt(xb[...], wd[1, part, :]).astype(BF16)
            grad_pair.append(remote(gsp.at[0, :, part], ghb.at[1, :, part], g_send.at[2 + i], g_recv.at[2 + i], pair))
            other = pl.ds(HID + i * (HID // 2), HID // 2)
            gsp[1, :, part] = (nt(xbn[...], wd[1, part, F2]) + gpn[:, other].astype(F32)).astype(BF16)
            grad_pair.append(remote(gsp.at[1, :, part], ghb.at[3, :, part], g_send.at[4 + i], g_recv.at[4 + i], pair))
    f_parts = []
    with jax.named_scope("out f part"):
        for h in range(2):
            part = pl.ds(h * HALF, HALF)
            fs[:, part] = pair_total(1, half(1, h)).astype(BF16)
            f_parts.append(remote(fs.at[:, part], fr.at[:, part], h_send.at[4 + h], h_recv.at[4 + h], next_pair))
    with jax.named_scope("gh pair wait"):
        for copy in grad_pair:
            copy.wait_recv()
    singles_p, firsts_p, firsts_n, summed = [], [], [], []
    with jax.named_scope("ring sums 0"):
        for r in (1, 3):
            grad_group(r)
        firsts_n.append(send_first_next(0))
        firsts_p.append(send_first_pair(0))
        singles_p.append(send_single_pair(0))
    with jax.named_scope("ring sums 1"):
        firsts_n.append(send_first_next(1))
        firsts_p.append(send_first_pair(1))
        singles_p.append(send_single_pair(1))
        firsts_p.append(send_first_pair(2))
        for q in range(2):
            own_parts(q)
    for h in range(2):
        with jax.named_scope(f"f part wait {h}"):
            f_parts[h].wait_recv()
        with jax.named_scope(f"out f 1 {h}"):
            stack_up(0, 1, h, pair_total(0, half(1, h)) + fr[:, h * HALF:(h + 1) * HALF].astype(F32))
            give_back_quarter(4 + h)
            if h == 0:
                own_parts(2)
                own_parts(3)
    for q in range(2):
        summed.append(send_sum(q))
    with jax.named_scope("first 2 3"):
        firsts_n.append(send_first_next(2))
        singles_p.append(send_single_pair(2))
        singles_n.append(send_single_next(2))
        firsts_p.append(send_first_pair(3))
        firsts_n.append(send_first_next(3))
    for q in range(2):
        finish_sum(q)
    summed.append(send_sum(2))
    singles_p.append(send_single_pair(3))
    singles_n.append(send_single_next(3))
    summed.append(send_sum(3))
    home_forward(0)
    finish_sum(2)
    home_forward(1)
    finish_sum(3)

    inner = home_backward(0)
    for q in range(1, 2 * NCH):
        inner = inner + home_backward(q)
    with jax.named_scope("final"):
        shift = inverse_b * inverse_b * jnp.sum(inner, axis=-1, keepdims=True) / D
        for q in range(2 * NCH):
            cols = quarters[q]
            out_b[:, cols] = (ret[:, cols].astype(F32) + inverse_b * (
                gnorm[:, cols] - kept[:, cols].astype(F32) * shift)).astype(BF16)

    for copy in pending:
        copy.wait_send()
    for i, c in ((0, 0), (0, 1), (1, 0), (1, 1), (2, 0)):
        whole(i, c).wait_send()
    for n in range(6):
        whole_quarter(n).wait_send()


def on_device(forward_inputs, forward_routes, forward_gates, backward_inputs, backward_cotangent, backward_routes,
              backward_gates, saved_preacts, norm_gain, gate_weight, up_weight, down_weight):
    vmem = pl.BlockSpec(memory_space=pltpu.VMEM)
    hbm = pl.BlockSpec(memory_space=pl.ANY)
    dma = pltpu.SemaphoreType.DMA
    out = pltpu.VMEM((TOK, D), BF16)
    scratch = [
        pltpu.VMEM((TOK, D), BF16),
        pltpu.VMEM((TOK, D), BF16),
        pltpu.VMEM((TOK, D), BF16),
        pltpu.VMEM((RING * ROWS, 2 * HID), BF16),
        pltpu.VMEM((D, HID), BF16),
        pltpu.VMEM((D, HID), BF16),
        pltpu.VMEM((RING, HID, D), BF16),
        pltpu.VMEM((2, PACK, NSUB * TOK), BF16),
        pltpu.VMEM((2, NSUB * TOK, PACK), BF16),
        pltpu.VMEM((PACK, NSUB * ROWS), BF16),
        pltpu.VMEM((NSUB * ROWS, PACK), BF16),
        pltpu.VMEM((1, TOK), jnp.int32),
        pltpu.VMEM((1, D), F32),
        pltpu.VMEM((TOK, D), BF16),
        pltpu.VMEM((4, NCH, PACK, 256), BF16),
        pltpu.VMEM((4, NCH, PACK, 256), BF16),
        pltpu.VMEM((RING, ROWS, D), BF16),
        pltpu.VMEM((ROWS, D), BF16),
        pltpu.VMEM((ROWS, 2 * HALF), BF16),
        pltpu.VMEM((2, ROWS, HID), BF16),
        pltpu.VMEM((2, ROWS, HID), BF16),
        pltpu.VMEM((2, ROWS, HID), BF16),
        pltpu.VMEM((2, ROWS, HID), BF16),
        pltpu.VMEM((ROWS, 2 * HALF), BF16),
        pltpu.VMEM((ROWS, 2 * HALF), BF16),
        pltpu.VMEM((ROWS, 2 * HID), BF16),
        pltpu.VMEM((ROWS, 2 * HID), BF16),
        pltpu.VMEM((2, ROWS, HID), BF16),
        pltpu.VMEM((RING, ROWS, HID), BF16),
        pltpu.VMEM((RING, ROWS, 2 * HID), F32),
        pltpu.VMEM((RING, ROWS, 2 * HID), BF16),
        pltpu.VMEM((3, ROWS, D), BF16),
        pltpu.VMEM((ROWS, D), F32),
        pltpu.VMEM((ROWS, D), F32),
        pltpu.VMEM((ROWS, D), BF16),
        pltpu.VMEM((ROWS, D), BF16),
        pltpu.VMEM((ROWS, D), BF16),
        pltpu.VMEM((2, NCH, NSUB * ROWS, 256), BF16),
        pltpu.VMEM((TOK, D), F32),
        dma((6,)), dma((4,)), dma((4,)), dma((8,)), dma((8,)), dma((8,)), dma((8,)), dma((12,)), dma((12,)),
        dma((6,)), dma((6,)), dma((6,)), dma((6,)), dma((24,)), dma((24,)), dma((6,)), dma((6,)),
    ]
    call = pl.pallas_call(
        kernel,
        out_shape=(out, out),
        in_specs=[hbm, hbm, hbm, vmem, vmem, vmem, vmem, hbm, vmem, hbm, hbm, hbm],
        out_specs=(vmem, vmem),
        scratch_shapes=scratch,
        compiler_params=pltpu.CompilerParams(collective_id=0, has_side_effects=True,
                                             vmem_limit_bytes=62 * 2 ** 20),
        cost_estimate=pl.CostEstimate(flops=10 ** 10, bytes_accessed=2 * 10 ** 7, transcendentals=10 ** 6),
    )

    def row(values):
        return values.reshape(1, TOK)

    outputs, grads = call(
        forward_inputs[0], backward_cotangent[0], backward_inputs[0], row(forward_routes), row(forward_gates),
        row(backward_routes), row(backward_gates), saved_preacts[0, 0], norm_gain, gate_weight[0], up_weight[0],
        down_weight[0])
    return outputs[None], grads[None]


def solution(mesh):
    tokens = P("pipe", "ep", None)
    in_specs = (tokens,) * 7 + (P("pipe", "ep", None, None), P("pipe", None), P("pipe", None, "ep"),
                                P("pipe", None, "ep"), tokens)
    return jax.shard_map(on_device, mesh=mesh, in_specs=in_specs, out_specs=(tokens, tokens), check_vma=False)
```
